512 devices in a mesh: replica: 64 (over z_hi, y, core), tensor: 8 (over x, z_lo).
Axes of the slice: x: 4, y: 8, z: 8 (z_hi: 4, z_lo: 2; z = z_hi * 2 + z_lo), core: 2. Of those that a mesh axis runs over, the one named last changes fastest.
Arguments:
- queries: bfloat16 [2048, 8192], P('replica', 'tensor'), may hold values from -130 to 130
- cache_keys: bfloat16 [2048, 8, 128, 128], P('replica', 'tensor'), may hold values from -6 to 6
- cache_values: bfloat16 [2048, 8, 128, 128], P('replica', 'tensor'), may hold values from -6 to 6
- new_keys: bfloat16 [2048, 1024], P('replica', 'tensor'), may hold values from -6 to 6
- new_values: bfloat16 [2048, 1024], P('replica', 'tensor'), may hold values from -6 to 6
- cache_lengths: int32 [2048], P('replica'), may hold values from 2 to 128, as said below
- residual: bfloat16 [2048, 8192], P('replica', 'tensor'), may hold values from -90 to 90
- norm_gain: float32 [8192], P('tensor'), may hold values from 0.1 to 1.9
- draft_input: bfloat16 [2048, 8192], P('replica', 'tensor'), may hold values from -90 to 90
- trainer_of: int32 [64], P('replica'), may hold values from 0 to 15
- factor_down: float32 [64, 8192], P(None, 'tensor'), may hold values from -5 to 5
- factor_up: float32 [64, 8192], P(None, 'tensor'), may hold values from -5 to 5
Outputs:
- hidden_rows: bfloat16 [2048, 8192], P('replica', 'tensor')
- draft_next: bfloat16 [2048, 8192], P('replica', 'tensor')
- new_down: float32 [64, 8192], P(None, 'tensor')
- new_up: float32 [64, 8192], P(None, 'tensor')
The draws below stay inside these ranges and needn't reach their ends.
Inputs may be any that keep to these rules, and one draw needn't show every extreme that they name: `cache_lengths`: every row has two or more live slots; some row has all 128.
All inputs are finite; a program needn't handle non-finite values.
Results may differ from the reference program's by a relative error of at most 0.0055.
Values sent between devices are 32-bit elements; how exact they have to be, the bound alone decides.
A program may use at most 64 MiB of HBM per device.

```python
import math
import jax
import jax.numpy as jnp
from jax import lax

D = 8192
HEADS = 64
KEY_VALUE_HEADS = 8
HEAD_SIZE = 128
RANK = 64
CACHE = 128
ROW_DEV = 32
ROWS = 2048
TRAINERS = 16
N_REPLICA = 64


def anchor_keys(key):
    return jax.random.truncated_normal(jax.random.fold_in(key, 5), -6.0, 6.0, (ROWS, KEY_VALUE_HEADS, HEAD_SIZE), jnp.float32)


def draw_cache_keys(key, part):
    anchor = anchor_keys(key)
    key = jax.random.fold_in(key, 11)
    keys = jax.random.truncated_normal(key, -6.0, 6.0, (ROWS, KEY_VALUE_HEADS, CACHE, HEAD_SIZE), jnp.float32)
    keys = keys.at[:, :, 0, :].set(anchor)
    return keys.astype(jnp.bfloat16)


def draw_queries(key, part):
    key = jax.random.fold_in(key, 12)
    base = jax.random.truncated_normal(key, -6.0, 6.0, (ROWS, HEADS, HEAD_SIZE), jnp.float32)
    return base.reshape(ROWS, HEADS * HEAD_SIZE).astype(jnp.bfloat16)


def draw_cache_lengths(key, part):
    key = jax.random.fold_in(key, 13)
    lengths = jax.random.randint(key, (ROWS,), 2, CACHE + 1, dtype=jnp.int32)
    return lengths.at[0].set(CACHE)


def draw_residual(key, part):
    key = jax.random.fold_in(key, 14)
    key_val, key_col = jax.random.split(key, 2)
    columns = jnp.exp(math.log(3.0) * jnp.arange(D, dtype=jnp.float32) / D)
    columns = columns * jnp.exp(jax.random.uniform(key_col, (D,), jnp.float32, -math.log(2.0), math.log(2.0)))
    values = jax.random.truncated_normal(key_val, -4.0, 4.0, (ROWS, D), jnp.float32)
    return (values * columns[None, :]).astype(jnp.bfloat16)


def draw_draft_input(key, part):
    key = jax.random.fold_in(key, 15)
    key_val, key_col = jax.random.split(key, 2)
    columns = jnp.exp(math.log(3.0) * jnp.arange(D, dtype=jnp.float32) / D)
    columns = columns * jnp.exp(jax.random.uniform(key_col, (D,), jnp.float32, -math.log(2.0), math.log(2.0)))
    values = jax.random.truncated_normal(key_val, -4.0, 4.0, (ROWS, D), jnp.float32)
    return (values * columns[None, :]).astype(jnp.bfloat16)


def with_ends(values, own_key, low, top_value):
    longest = values.shape.index(max(values.shape))
    spots = []
    for shift in (0, 1):
        where = [jax.random.randint(jax.random.fold_in(own_key, axis), (), 0, length) for axis, length in enumerate(values.shape)]
        where[longest] = (where[longest] + shift) % values.shape[longest]
        spots.append(tuple(where))
    return values.at[spots[0]].set(low).at[spots[1]].set(top_value)


def steps_of(key, dims, cuts, smallest, high):
    def one(dim, shards_of):
        steps = jax.random.uniform(jax.random.fold_in(jax.random.fold_in(key, 6), dim), (shards_of,), jnp.float32, smallest / len(cuts), high / len(cuts))
        return jnp.repeat(jnp.exp(steps), dims[dim] // shards_of).reshape((-1,) + (1,) * (len(dims) - dim - 1))

    level = one(*cuts[0])
    for cut in cuts[1:]:
        level = level * one(*cut)
    return level


def normal_values(key, shape, deviation, most, cuts=(), held_as=jnp.bfloat16):
    entries = jax.random.normal(key, shape, jnp.float32) * deviation
    if len(cuts) > 0:
        entries = steps_of(key, shape, cuts, -0.22, 0.18) * entries
    return jnp.clip(entries, min=-most, max=most).astype(held_as)


def setup_inputs(seed: int = 0) -> dict:
    key_of = jax.random.split(jax.random.key(seed), 13)
    queries = draw_queries(jax.random.fold_in(key_of[12], 71), 0)
    cache_keys = draw_cache_keys(jax.random.fold_in(key_of[12], 71), 0)
    cache_values = normal_values(key_of[2], (ROWS, KEY_VALUE_HEADS, CACHE, HEAD_SIZE), 1.0, 6.0, ((0, 64), (1, 8)))
    new_keys = normal_values(key_of[3], (ROWS, KEY_VALUE_HEADS * HEAD_SIZE), 1.0, 6.0, ((0, 64), (1, 8)))
    new_values = normal_values(key_of[4], (ROWS, KEY_VALUE_HEADS * HEAD_SIZE), 1.0, 6.0, ((0, 64), (1, 8)))
    cache_lengths = draw_cache_lengths(jax.random.fold_in(key_of[12], 71), 0)
    residual = draw_residual(jax.random.fold_in(key_of[12], 71), 0)
    norm_gain = jnp.clip(1.0 + 0.18 * jax.random.normal(key_of[7], (D,), jnp.float32), 0.1, 1.9)
    draft_input = draw_draft_input(jax.random.fold_in(key_of[12], 71), 0)
    trainer_of = with_ends(jax.random.randint(key_of[9], (N_REPLICA,), 0, TRAINERS), jax.random.fold_in(key_of[9], 1), 0, TRAINERS - 1).astype(jnp.int32)
    factor_down = normal_values(key_of[10], (RANK, D), 1.0, 5.0, ((1, 8),), jnp.float32)
    factor_up = normal_values(key_of[11], (RANK, D), 1.0, 5.0, ((1, 8),), jnp.float32)
    return {"queries": queries, "cache_keys": cache_keys, "cache_values": cache_values, "new_keys": new_keys, "new_values": new_values, "cache_lengths": cache_lengths, "residual": residual, "norm_gain": norm_gain, "draft_input": draft_input, "trainer_of": trainer_of, "factor_down": factor_down, "factor_up": factor_up}


def attend_block(block):
    query, keys, values, current_key, own_value, lengths = block
    token_count = query.shape[0]
    group = HEADS // KEY_VALUE_HEADS
    score_scale = 1.0 / math.sqrt(HEAD_SIZE)
    query_float = query.astype(jnp.float32).reshape(token_count, KEY_VALUE_HEADS, group, HEAD_SIZE)
    scores = jnp.einsum('bkgd,bkpd->bkgp', query_float, keys.astype(jnp.float32)) * score_scale
    own_scores = jnp.einsum('romy,roy->rom', query_float, current_key.astype(jnp.float32).reshape(token_count, KEY_VALUE_HEADS, HEAD_SIZE)) * score_scale
    live = jnp.arange(CACHE, dtype=jnp.int32)[None, :] < lengths[:, None]
    scores = jnp.where(live[:, None, None, :], scores, -jnp.inf)
    top = jnp.maximum(lax.optimization_barrier(jnp.max(scores, axis=-1)), own_scores)
    weights = jnp.exp(scores - top[..., None])
    own_weight = jnp.exp(own_scores - top)
    total = lax.optimization_barrier(jnp.sum(weights, axis=-1)) + own_weight
    probs = (weights / total[..., None]).astype(jnp.bfloat16)
    own_prob = (own_weight / total).astype(jnp.bfloat16)
    context = jnp.einsum('bkgp,bkpd->bkgd', probs.astype(jnp.float32), values.astype(jnp.float32))
    context = context + own_prob.astype(jnp.float32)[..., None] * own_value.astype(jnp.float32).reshape(token_count, KEY_VALUE_HEADS, 1, HEAD_SIZE)
    return context.reshape(token_count, HEADS * HEAD_SIZE)

def reference(queries, cache_keys, cache_values, new_keys, new_values, cache_lengths, residual, norm_gain, draft_input, trainer_of, factor_down, factor_up):
    blocks = ROWS // ROW_DEV
    packed = (queries.reshape(blocks, ROW_DEV, D), cache_keys.reshape(blocks, ROW_DEV, KEY_VALUE_HEADS, CACHE, HEAD_SIZE), cache_values.reshape(blocks, ROW_DEV, KEY_VALUE_HEADS, CACHE, HEAD_SIZE), new_keys.reshape(blocks, ROW_DEV, KEY_VALUE_HEADS * HEAD_SIZE), new_values.reshape(blocks, ROW_DEV, KEY_VALUE_HEADS * HEAD_SIZE), cache_lengths.reshape(blocks, ROW_DEV))
    context = lax.map(attend_block, packed).reshape(ROWS, D)
    feature = residual.astype(jnp.float32) + context
    mean_sq = lax.optimization_barrier(jnp.mean(feature * feature, axis=1, keepdims=True))
    hidden_rows = (feature * lax.rsqrt(mean_sq + 1e-05) * norm_gain[None, :]).astype(jnp.bfloat16)
    down_b = factor_down.astype(jnp.bfloat16)
    up_b = factor_up.astype(jnp.bfloat16)
    root_width = 1.0 / math.sqrt(D)
    coef = 0.5 / math.sqrt(RANK)
    adapter = (jnp.dot(draft_input, down_b.T, preferred_element_type=jnp.float32) * root_width).astype(jnp.bfloat16)
    pred = draft_input.astype(jnp.float32) + coef * jnp.dot(adapter, up_b, preferred_element_type=jnp.float32)
    onehot = (trainer_of[:, None] == jnp.arange(TRAINERS, dtype=jnp.int32)[None, :]).astype(jnp.float32)
    loads = lax.optimization_barrier(jnp.sum(onehot, axis=0))
    own_load = lax.optimization_barrier(jnp.sum(onehot * loads[None, :], axis=1))
    weight = jnp.repeat(1.0 / (ROW_DEV * own_load), ROW_DEV)
    resid_grad = (weight[:, None] * (pred - hidden_rows.astype(jnp.float32))).astype(jnp.bfloat16)
    grad_up = coef * jnp.dot(adapter.T, resid_grad, preferred_element_type=jnp.float32)
    back = (coef * jnp.dot(resid_grad, up_b.T, preferred_element_type=jnp.float32)).astype(jnp.bfloat16)
    grad_down = jnp.dot(back.T, draft_input, preferred_element_type=jnp.float32) * root_width
    total_sq = jnp.sum(grad_down * grad_down) + jnp.sum(grad_up * grad_up)
    score_scale = jnp.sqrt(total_sq / (2.0 * RANK * D) + 1e-06)
    new_down = factor_down - 0.5 * grad_down / score_scale
    new_up = factor_up - 0.5 * grad_up / score_scale
    serve = (jnp.dot(hidden_rows, down_b.T, preferred_element_type=jnp.float32) * root_width).astype(jnp.bfloat16)
    draft_next = (hidden_rows.astype(jnp.float32) + coef * jnp.dot(serve, up_b, preferred_element_type=jnp.float32)).astype(jnp.bfloat16)
    return (hidden_rows, draft_next, new_down, new_up)
```

```python
import functools
import math

import jax
import jax.numpy as jnp
from jax import lax
from jax.experimental import pallas as pl
from jax.experimental.pallas import tpu as pltpu
from jax.sharding import PartitionSpec as P

D = 8192
RANK = 64
ROWS = 32
GROUP = 8
SIZE = 128
WIDTH = 1024
NT = 8
NY = 8
NZ = 4
NYC = 16
ROOT = 1.0 / math.sqrt(D)
COEF = 0.5 / math.sqrt(RANK)
MESH = pl.DeviceIdType.MESH
BF = jnp.bfloat16
F32 = jnp.float32
EXACT = lax.Precision.HIGHEST


def iota(shape, dim):
    return lax.broadcasted_iota(jnp.int32, shape, dim)


def dot_t(a, b):
    return lax.dot_general(a, b, (((1,), (1,)), ((), ())), preferred_element_type=F32)


def dot_rows(a, b):
    return lax.dot_general(a, b, (((0,), (0,)), ((), ())), preferred_element_type=F32)


def remote(src, dst, send_sem, recv_sem, device):
    return pltpu.make_async_remote_copy(
        src_ref=src,
        dst_ref=dst,
        send_sem=send_sem,
        recv_sem=recv_sem,
        device_id=device,
        device_id_type=MESH,
    )


def kernel(
    q_hbm, ck_hbm, cv_hbm, nk_hbm, nv_hbm, len_hbm, res_hbm, gain_hbm, dr_hbm, tr_hbm, fd_hbm, fu_hbm,
    hid_hbm, dn_hbm, nd_hbm, nu_hbm,
    q_v, ck_v, cv_v, nk_v, nv_v, len_v, res_v, gain_v, dr_v, tr_v, fd_v, fu_v,
    hid_v, dn_v, nd_v, nu_v,
    w_b, q3, ctx3, fg_b,
    slices, t_buf, r_buf, x_buf, late, l_buf, c_buf, z_buf, grads, s_t, s_y,
    in_sem, out_sem,
    t_ss, t_rs, r_ss, r_rs, x_ss, x_rs, l_ss, l_rs, c_ss, c_rs, z_ss, z_rs, g_ss, g_rs, f_ss, f_rs,
    st_ss, st_rs, sy_ss, sy_rs,
):
    r = lax.axis_index("replica")
    t = lax.axis_index("tensor")
    yc = lax.rem(r, NYC)
    z = r // NYC
    y = yc // 2
    c = lax.rem(yc, 2)
    sibling = (z * NYC + y * 2 + (1 - c), t)
    t_peers = [lax.rem(t + o, NT) for o in range(1, NT)]
    yc_peers = [lax.rem(yc + o, NYC) for o in range(1, NYC)]
    z_peers = [lax.rem(z + o, NZ) for o in range(1, NZ)]
    y_peers = [lax.rem(y + o, NY) for o in range(1, NY)]

    barrier = pltpu.get_barrier_semaphore()
    everyone = (
        [(r, p) for p in t_peers]
        + [(z * NYC + p, t) for p in yc_peers]
        + [(p * NYC + yc, t) for p in z_peers]
    )
    for device in everyone:
        pl.semaphore_signal(barrier, inc=1, device_id=device, device_id_type=MESH)

    loads = [
        pltpu.make_async_copy(src, dst, in_sem.at[i])
        for i, (src, dst) in enumerate(
            (
                (fd_hbm, fd_v), (fu_hbm, fu_v), (dr_hbm, dr_v), (q_hbm, q_v), (nk_hbm, nk_v), (len_hbm, len_v),
                (ck_hbm, ck_v), (nv_hbm, nv_v), (res_hbm, res_v), (gain_hbm, gain_v), (tr_hbm, tr_v), (cv_hbm, cv_v),
            )
        )
    ]
    for load in loads:
        load.start()
    for load in loads[:3]:
        load.wait()

    w_b[0:RANK, :] = fd_v[...].astype(BF)
    w_b[RANK:, :] = fu_v[...].astype(BF)
    draft_part = dot_t(dr_v[...], w_b[...])
    up_part = dot_t(w_b[RANK:, :], w_b[...])
    for g in range(GROUP):
        slices[0, g] = dr_v[:, g * SIZE : (g + 1) * SIZE].astype(F32)

    for load in loads[3:6]:
        load.wait()
    for g in range(GROUP):
        q3[pl.ds(g, ROWS, stride=GROUP), :] = q_v[:, g * SIZE : (g + 1) * SIZE].astype(F32)
    pick = (iota((ROWS * GROUP, ROWS), 0) // GROUP == iota((ROWS * GROUP, ROWS), 1)).astype(F32)
    own_key = jnp.dot(pick.astype(BF), nk_v[...], preferred_element_type=F32)
    lengths = jnp.dot(
        (pick * len_v[...].astype(F32)).astype(BF), jnp.ones((ROWS, SIZE), BF), preferred_element_type=F32
    )
    queries = q3[...]
    scale = 1.0 / math.sqrt(SIZE)
    own_score = jnp.sum(queries * own_key, axis=1, keepdims=True) * scale
    loads[6].wait()
    scores = lax.dot_general(
        queries.reshape(ROWS, GROUP, SIZE).astype(BF),
        ck_v[...],
        (((2,), (2,)), ((0,), (0,))),
        preferred_element_type=F32,
    ).reshape(ROWS * GROUP, SIZE)
    live = iota((ROWS * GROUP, SIZE), 1).astype(F32) < lengths
    scores = jnp.where(live, scores * scale, -jnp.inf)
    top = jnp.maximum(jnp.max(scores, axis=1, keepdims=True), own_score)
    weights = jnp.exp(scores - top)
    own_weight = jnp.exp(own_score - top)
    total = jnp.sum(weights, axis=1, keepdims=True) + own_weight
    probs = (weights / total).astype(BF)
    own_prob = (own_weight / total).astype(BF).astype(F32)
    for load in loads[7:]:
        load.wait()
    own_value = jnp.dot(pick.astype(BF), nv_v[...], preferred_element_type=F32)
    context = lax.dot_general(
        probs.reshape(ROWS, GROUP, SIZE),
        cv_v[...],
        (((2,), (1,)), ((0,), (0,))),
        preferred_element_type=F32,
    ).reshape(ROWS * GROUP, SIZE)
    ctx3[...] = context + own_prob * own_value

    squares = jnp.zeros((ROWS, SIZE), F32)
    for g in range(GROUP):
        cols = slice(g * SIZE, (g + 1) * SIZE)
        feature = res_v[:, cols].astype(F32) + ctx3[pl.ds(g, ROWS, stride=GROUP), :]
        squares = squares + feature * feature
        gained = feature * gain_v[:, cols]
        slices[1, g] = gained
        fg_b[:, cols] = gained.astype(BF)
    square_col = jnp.sum(squares, axis=1, keepdims=True)
    eye = iota((ROWS, SIZE), 0) == iota((ROWS, SIZE), 1)
    square_row = jnp.sum(jnp.where(eye, square_col, 0.0), axis=0, keepdims=True)
    feature_part = dot_t(fg_b[...], w_b[...])
    low = iota((ROWS, SIZE), 1) < RANK

    t_buf[t, 0:32, :] = draft_part
    t_buf[t, 32:64, :] = jnp.where(low, feature_part, up_part[0:32])
    t_buf[t, 64:96, :] = jnp.where(low, pltpu.roll(feature_part, RANK, 1), up_part[32:64])
    t_buf[t, 96:104, :] = jnp.broadcast_to(square_row, (8, SIZE))
    onehot = (iota((1, SIZE), 1) == tr_v[...]).astype(F32)
    c_buf[z] = onehot
    r_buf[yc] = slices[c, y]

    pl.semaphore_wait(barrier, len(everyone))

    sent = []

    def send(src, dst, ss, rs, device):
        copy = remote(src, dst, ss, rs, device)
        copy.start()
        sent.append(copy)

    for i, p in enumerate(z_peers):
        send(c_buf.at[z], c_buf.at[z], c_ss.at[i], c_rs.at[z], (p * NYC + yc, t))
    for i, p in enumerate(t_peers):
        send(t_buf.at[t], t_buf.at[t], t_ss.at[i], t_rs.at[t], (r, p))
    for i, p in enumerate(yc_peers):
        send(slices.at[lax.rem(p, 2), p // 2], r_buf.at[yc], r_ss.at[i], r_rs.at[yc], (z * NYC + p, t))

    for i, p in enumerate(z_peers):
        remote(c_buf.at[p], c_buf.at[p], c_ss.at[i], c_rs.at[p], (p * NYC + yc, t)).wait_recv()
    counts = c_buf[0] + c_buf[1] + c_buf[2] + c_buf[3]
    for i, p in enumerate(t_peers):
        remote(t_buf.at[p], t_buf.at[p], t_ss.at[i], t_rs.at[p], (r, p)).wait_recv()
    summed = t_buf[0]
    for p in range(1, NT):
        summed = summed + t_buf[p]
    square_all = summed[96:97]
    rs_row = lax.rsqrt(square_all * (1.0 / D) + 1e-05)
    rs_col = jnp.sum(jnp.where(eye, rs_row, 0.0), axis=1, keepdims=True)
    adapter = (summed[0:32] * ROOT).astype(BF).astype(F32)
    spread = jnp.dot(adapter[:, 0:RANK], summed[32:96], precision=EXACT, preferred_element_type=F32)
    back = COEF * (summed[0:32] + COEF * spread - rs_col * pltpu.roll(summed[64:96], RANK, 1))
    low16 = low[0:16]
    row8 = iota((8, SIZE), 0)
    extra = jnp.where(row8 == 0, rs_row, jnp.where(row8 == 1, counts, jnp.where(row8 == 2, onehot, 0.0)))
    late[0, 0:16, :] = jnp.where(low16, pltpu.roll(back[0:16], RANK, 1), back[16:32])
    late[1, 0:16, :] = jnp.where(low16, adapter[0:16], pltpu.roll(adapter[16:32], RANK, 1))
    late[0, 16:24, :] = extra
    late[1, 16:24, :] = extra
    for i, p in enumerate(yc_peers):
        send(late.at[lax.rem(p, 2)], l_buf.at[yc], l_ss.at[i], l_rs.at[yc], (z * NYC + p, t))
    l_buf[yc] = late[c]

    serve = (summed[32:64] * rs_col * ROOT).astype(BF)
    drafted = jnp.dot(serve[:, 0:RANK], w_b[RANK:, :], preferred_element_type=F32)
    for g in range(GROUP):
        cols = slice(g * SIZE, (g + 1) * SIZE)
        hidden = (slices[1, g] * rs_col).astype(BF)
        hid_v[:, cols] = hidden
        dn_v[:, cols] = (hidden.astype(F32) + COEF * drafted[:, cols]).astype(BF)
    stores = [
        pltpu.make_async_copy(hid_v, hid_hbm, out_sem.at[0]),
        pltpu.make_async_copy(dn_v, dn_hbm, out_sem.at[1]),
    ]
    for store in stores:
        store.start()

    for i, p in enumerate(yc_peers):
        remote(r_buf.at[p], r_buf.at[p], r_ss.at[i], r_rs.at[p], (z * NYC + p, t)).wait_recv()
    swap = remote(r_buf, x_buf, x_ss, x_rs, sibling)
    swap.start()
    sent.append(swap)
    swap.wait_recv()
    for i, p in enumerate(yc_peers):
        remote(l_buf.at[p], l_buf.at[p], l_ss.at[i], l_rs.at[p], (z * NYC + p, t)).wait_recv()

    packed = l_buf[:, 0:16, :].reshape(256, SIZE)
    tiles = l_buf[:, 16:24, :]
    load_all = jnp.sum(tiles, axis=0)[1:2, :]
    tile_loads = jnp.sum(tiles * load_all[None], axis=2, keepdims=True)
    tile_loads = jnp.broadcast_to(tile_loads, (NYC, 8, SIZE)).reshape(SIZE, SIZE)
    first = (iota((256, SIZE), 0) // 16) * 8
    lane = iota((256, SIZE), 1)
    load_rows = jnp.dot(
        (lane == first + 2).astype(F32), tile_loads, precision=EXACT, preferred_element_type=F32
    )
    weight = 1.0 / (ROWS * load_rows)

    @pl.when(c == 0)
    def _():
        left = (packed * weight).astype(BF)
        top_rows = r_buf[:, 0:16, :].reshape(256, SIZE).astype(BF)
        bottom_rows = r_buf[:, 16:32, :].reshape(256, SIZE).astype(BF)
        z_buf[z] = (dot_rows(left, top_rows)[0:RANK] + dot_rows(left, bottom_rows)[RANK:]) * ROOT

    @pl.when(c == 1)
    def _():
        left = packed.astype(BF)
        up = w_b[RANK:, pl.ds(pl.multiple_of(y * SIZE, SIZE), SIZE)]
        none = jnp.zeros_like(up)
        rs_all = jnp.dot(
            (lane == first).astype(F32), tiles.reshape(SIZE, SIZE), precision=EXACT, preferred_element_type=F32
        )
        place = lax.rem(iota((256, SIZE), 0), 16)

        def half(h, up_half):
            rs = jnp.sum(jnp.where(lane == place + 16 * h, rs_all, 0.0), axis=1, keepdims=True)
            rows = slice(16 * h, 16 * h + 16)
            drafts = x_buf[:, rows, :].reshape(256, SIZE)
            gained = r_buf[:, rows, :].reshape(256, SIZE)
            lift = jnp.dot(left, up_half, preferred_element_type=F32)
            resid = (weight * (drafts + COEF * lift - rs * gained)).astype(BF)
            return dot_rows(left, resid)

        top_part = half(0, jnp.concatenate([up, none], axis=0))
        bottom_part = half(1, jnp.concatenate([none, up], axis=0))
        z_buf[z] = (top_part[0:RANK] + bottom_part[RANK:]) * COEF

    for i, p in enumerate(z_peers):
        send(z_buf.at[z], z_buf.at[z], z_ss.at[i], z_rs.at[z], (p * NYC + yc, t))
    for i, p in enumerate(z_peers):
        remote(z_buf.at[p], z_buf.at[p], z_ss.at[i], z_rs.at[p], (p * NYC + yc, t)).wait_recv()
    grad = z_buf[0] + z_buf[1] + z_buf[2] + z_buf[3]
    grads[c, y] = grad

    for i, p in enumerate(y_peers):
        send(grads.at[c, y], grads.at[c, y], g_ss.at[i], g_rs.at[y], (z * NYC + p * 2 + c, t))
    s_t[t] = jnp.sum(grad * grad, axis=0, keepdims=True)
    for i, p in enumerate(t_peers):
        send(s_t.at[t], s_t.at[t], st_ss.at[i], st_rs.at[t], (r, p))
    send(grads.at[c, y], grads.at[c, y], f_ss.at[y], f_rs.at[y], sibling)
    for i, p in enumerate(t_peers):
        remote(s_t.at[p], s_t.at[p], st_ss.at[i], st_rs.at[p], (r, p)).wait_recv()
    part = s_t[0]
    for p in range(1, NT):
        part = part + s_t[p]
    s_y[yc] = part
    for i, p in enumerate(yc_peers):
        send(s_y.at[yc], s_y.at[yc], sy_ss.at[i], sy_rs.at[yc], (z * NYC + p, t))
    for o in (1, 7, 2, 6, 3, 5, 4):
        p = lax.rem(y + o, NY)
        remote(grads.at[c, p], grads.at[c, p], g_ss.at[o - 1], g_rs.at[p], (z * NYC + p * 2 + c, t)).wait_recv()
        send(grads.at[c, p], grads.at[c, p], f_ss.at[p], f_rs.at[p], sibling)
    for i, p in enumerate(yc_peers):
        remote(s_y.at[p], s_y.at[p], sy_ss.at[i], sy_rs.at[p], (z * NYC + p, t)).wait_recv()
    whole = s_y[0]
    for p in range(1, NYC):
        whole = whole + s_y[p]
    total_sq = jnp.sum(whole, axis=1, keepdims=True)
    step = 0.5 / jnp.sqrt(total_sq * (1.0 / (2.0 * RANK * D)) + 1e-06)
    for p in range(NY):
        remote(grads.at[1 - c, p], grads.at[1 - c, p], f_ss.at[p], f_rs.at[p], sibling).wait_recv()
    for p in range(NY):
        cols = slice(p * SIZE, (p + 1) * SIZE)
        nd_v[:, cols] = fd_v[:, cols] - grads[0, p] * step
        nu_v[:, cols] = fu_v[:, cols] - grads[1, p] * step
    stores += [
        pltpu.make_async_copy(nd_v, nd_hbm, out_sem.at[2]),
        pltpu.make_async_copy(nu_v, nu_hbm, out_sem.at[3]),
    ]
    for store in stores[2:]:
        store.start()
    for copy in sent:
        copy.wait_send()
    for store in stores:
        store.wait()


def local(
    queries,
    cache_keys,
    cache_values,
    new_keys,
    new_values,
    cache_lengths,
    residual,
    norm_gain,
    draft_input,
    trainer_of,
    factor_down,
    factor_up,
):
    inputs = (
        queries,
        cache_keys.reshape(ROWS, SIZE, SIZE),
        cache_values.reshape(ROWS, SIZE, SIZE),
        new_keys,
        new_values,
        cache_lengths.reshape(1, ROWS),
        residual,
        norm_gain.reshape(1, WIDTH),
        draft_input,
        trainer_of.reshape(1, 1),
        factor_down,
        factor_up,
    )
    outs = (
        jax.ShapeDtypeStruct((ROWS, WIDTH), BF),
        jax.ShapeDtypeStruct((ROWS, WIDTH), BF),
        jax.ShapeDtypeStruct((RANK, WIDTH), F32),
        jax.ShapeDtypeStruct((RANK, WIDTH), F32),
    )
    vmem = pltpu.VMEM
    dma = pltpu.SemaphoreType.DMA
    scratch = (
        [vmem(a.shape, a.dtype) for a in inputs]
        + [vmem(a.shape, a.dtype) for a in outs]
        + [
            vmem((2 * RANK, WIDTH), BF),
            vmem((ROWS * GROUP, SIZE), F32),
            vmem((ROWS * GROUP, SIZE), F32),
            vmem((ROWS, WIDTH), BF),
            vmem((2, NY, ROWS, SIZE), F32),
            vmem((NT, 104, SIZE), F32),
            vmem((NYC, ROWS, SIZE), F32),
            vmem((NYC, ROWS, SIZE), F32),
            vmem((2, 24, SIZE), F32),
            vmem((NYC, 24, SIZE), F32),
            vmem((NZ, 1, SIZE), F32),
            vmem((NZ, RANK, SIZE), F32),
            vmem((2, NY, RANK, SIZE), F32),
            vmem((NT, 1, SIZE), F32),
            vmem((NYC, 1, SIZE), F32),
            dma((len(inputs),)),
            dma((len(outs),)),
            dma((NT - 1,)), dma((NT,)),
            dma((NYC - 1,)), dma((NYC,)),
            dma, dma,
            dma((NYC - 1,)), dma((NYC,)),
            dma((NZ - 1,)), dma((NZ,)),
            dma((NZ - 1,)), dma((NZ,)),
            dma((NY - 1,)), dma((NY,)),
            dma((NY,)), dma((NY,)),
            dma((NT - 1,)), dma((NT,)),
            dma((NYC - 1,)), dma((NYC,)),
        ]
    )
    anywhere = pl.BlockSpec(memory_space=pl.ANY)
    return pl.pallas_call(
        kernel,
        out_shape=outs,
        in_specs=[anywhere] * len(inputs),
        out_specs=tuple([anywhere] * len(outs)),
        scratch_shapes=scratch,
        compiler_params=pltpu.CompilerParams(
            collective_id=0, has_side_effects=True, vmem_limit_bytes=24 * 1024 * 1024
        ),
        name="decode_and_draft",
    )(*inputs)


def solution(mesh):
    return jax.shard_map(
        local,
        mesh=mesh,
        in_specs=(
            P("replica", "tensor"),
            P("replica", "tensor", None, None),
            P("replica", "tensor", None, None),
            P("replica", "tensor"),
            P("replica", "tensor"),
            P("replica"),
            P("replica", "tensor"),
            P("tensor"),
            P("replica", "tensor"),
            P("replica"),
            P(None, "tensor"),
            P(None, "tensor"),
        ),
        out_specs=(
            P("replica", "tensor"),
            P("replica", "tensor"),
            P(None, "tensor"),
            P(None, "tensor"),
        ),
        check_vma=False,
    )
```

```python
import functools
import math

import jax
import jax.numpy as jnp
from jax import lax
from jax.experimental import pallas as pl
from jax.experimental.pallas import tpu as pltpu
from jax.sharding import PartitionSpec as P

D = 8192
RANK = 64
ROWS = 32
GROUP = 8
SIZE = 128
WIDTH = 1024
NT = 8
NY = 8
NZ = 4
NYC = 16
ROOT = 1.0 / math.sqrt(D)
COEF = 0.5 / math.sqrt(RANK)
MESH = pl.DeviceIdType.MESH
BF = jnp.bfloat16
F32 = jnp.float32
EXACT = lax.Precision.HIGHEST


def iota(shape, dim):
    return lax.broadcasted_iota(jnp.int32, shape, dim)


def dot_t(a, b):
    return lax.dot_general(a, b, (((1,), (1,)), ((), ())), preferred_element_type=F32)


def dot_rows(a, b):
    return lax.dot_general(a, b, (((0,), (0,)), ((), ())), preferred_element_type=F32)


def remote(src, dst, send_sem, recv_sem, device):
    return pltpu.make_async_remote_copy(
        src_ref=src,
        dst_ref=dst,
        send_sem=send_sem,
        recv_sem=recv_sem,
        device_id=device,
        device_id_type=MESH,
    )


def kernel(
    q_hbm, ck_hbm, cv_hbm, nk_hbm, nv_hbm, len_hbm, res_hbm, gain_hbm, dr_hbm, tr_hbm, fd_hbm, fu_hbm,
    hid_hbm, dn_hbm, nd_hbm, nu_hbm,
    q_v, ck_v, cv_v, nk_v, nv_v, len_v, res_v, gain_v, dr_v, tr_v, fd_v, fu_v,
    hid_v, dn_v, nd_v, nu_v,
    w_b, q3, ctx3, fg_b,
    slices, t_buf, r_buf, x_buf, late, l_buf, c_buf, z_buf, grads, s_t, s_y,
    in_sem, out_sem, send_sem, recv_sem, slice_sem,
):
    r = lax.axis_index("replica")
    t = lax.axis_index("tensor")
    yc = lax.rem(r, NYC)
    z = r // NYC
    y = yc // 2
    c = lax.rem(yc, 2)
    x = t // 2
    low_z = lax.rem(t, 2)
    y_order = (4, 3, 5, 2, 6, 1, 7)
    t_peers = [
        lax.rem(x + dx, 4) * 2 + lax.rem(low_z + dz, 2)
        for dx, dz in ((2, 1), (1, 1), (3, 1), (2, 0), (1, 0), (3, 0), (0, 1))
    ]
    yc_peers = [lax.rem(y + dy, NY) * 2 + lax.rem(c + dc, 2) for dy in y_order for dc in (0, 1)]
    yc_peers = yc_peers + [y * 2 + 1 - c]
    z_peers = [lax.rem(z + dz, NZ) for dz in (2, 1, 3)]
    y_peers = [lax.rem(y + dy, NY) for dy in y_order]

    def at_t(p):
        return (r, p)

    def at_yc(p):
        return (z * NYC + p, t)

    def at_z(p):
        return (p * NYC + yc, t)

    sibling = at_yc(y * 2 + 1 - c)

    barrier = pltpu.get_barrier_semaphore()
    everyone = (
        [at_t(p) for p in t_peers]
        + [at_yc(p) for p in yc_peers]
        + [at_z(p) for p in z_peers]
        + [(z * NYC + y * 2 + 1 - c, p) for p in t_peers]
    )
    for device in everyone:
        pl.semaphore_signal(barrier, inc=1, device_id=device, device_id_type=MESH)

    loads = [
        pltpu.make_async_copy(src, dst, in_sem.at[i])
        for i, (src, dst) in enumerate(
            (
                (fd_hbm, fd_v), (fu_hbm, fu_v), (dr_hbm, dr_v), (q_hbm, q_v), (nk_hbm, nk_v), (len_hbm, len_v),
                (ck_hbm, ck_v), (nv_hbm, nv_v), (res_hbm, res_v), (gain_hbm, gain_v), (tr_hbm, tr_v), (cv_hbm, cv_v),
            )
        )
    ]
    for load in loads:
        load.start()
    for load in loads[:3]:
        load.wait()

    w_b[0:RANK, :] = fd_v[...].astype(BF)
    w_b[RANK:, :] = fu_v[...].astype(BF)
    draft_part = dot_t(dr_v[...], w_b[...])
    up_part = dot_t(w_b[RANK:, :], w_b[...])
    for g in range(GROUP):
        slices[0, g] = dr_v[:, g * SIZE : (g + 1) * SIZE].astype(F32)

    for load in loads[3:6]:
        load.wait()
    for g in range(GROUP):
        q3[pl.ds(g, ROWS, stride=GROUP), :] = q_v[:, g * SIZE : (g + 1) * SIZE].astype(F32)
    pick = (iota((ROWS * GROUP, ROWS), 0) // GROUP == iota((ROWS * GROUP, ROWS), 1)).astype(F32)
    own_key = jnp.dot(pick.astype(BF), nk_v[...], preferred_element_type=F32)
    lengths = jnp.dot(
        (pick * len_v[...].astype(F32)).astype(BF), jnp.ones((ROWS, SIZE), BF), preferred_element_type=F32
    )
    queries = q3[...]
    scale = 1.0 / math.sqrt(SIZE)
    own_score = jnp.sum(queries * own_key, axis=1, keepdims=True) * scale
    loads[6].wait()
    scores = lax.dot_general(
        queries.reshape(ROWS, GROUP, SIZE).astype(BF),
        ck_v[...],
        (((2,), (2,)), ((0,), (0,))),
        preferred_element_type=F32,
    ).reshape(ROWS * GROUP, SIZE)
    live = iota((ROWS * GROUP, SIZE), 1).astype(F32) < lengths
    scores = jnp.where(live, scores * scale, -jnp.inf)
    top = jnp.maximum(jnp.max(scores, axis=1, keepdims=True), own_score)
    weights = jnp.exp(scores - top)
    own_weight = jnp.exp(own_score - top)
    total = jnp.sum(weights, axis=1, keepdims=True) + own_weight
    probs = (weights / total).astype(BF)
    own_prob = (own_weight / total).astype(BF).astype(F32)
    for load in loads[7:]:
        load.wait()
    own_value = jnp.dot(pick.astype(BF), nv_v[...], preferred_element_type=F32)
    context = lax.dot_general(
        probs.reshape(ROWS, GROUP, SIZE),
        cv_v[...],
        (((2,), (1,)), ((0,), (0,))),
        preferred_element_type=F32,
    ).reshape(ROWS * GROUP, SIZE)
    ctx3[...] = context + own_prob * own_value

    squares = jnp.zeros((ROWS, SIZE), F32)
    for g in range(GROUP):
        cols = slice(g * SIZE, (g + 1) * SIZE)
        feature = res_v[:, cols].astype(F32) + ctx3[pl.ds(g, ROWS, stride=GROUP), :]
        squares = squares + feature * feature
        gained = feature * gain_v[:, cols]
        slices[1, g] = gained
        fg_b[:, cols] = gained.astype(BF)
    square_col = jnp.sum(squares, axis=1, keepdims=True)
    eye = iota((ROWS, SIZE), 0) == iota((ROWS, SIZE), 1)
    square_row = jnp.sum(jnp.where(eye, square_col, 0.0), axis=0, keepdims=True)
    feature_part = dot_t(fg_b[...], w_b[...])
    low = iota((ROWS, SIZE), 1) < RANK

    t_buf[t, 0:32, :] = draft_part
    t_buf[t, 32:64, :] = jnp.where(low, feature_part, up_part[0:32])
    t_buf[t, 64:96, :] = jnp.where(low, pltpu.roll(feature_part, RANK, 1), up_part[32:64])
    t_buf[t, 96:104, :] = jnp.broadcast_to(square_row, (8, SIZE))
    onehot = (iota((1, SIZE), 1) == tr_v[...] + 64).astype(F32)
    c_buf[z] = onehot
    r_buf[yc] = slices[c, y]

    pl.semaphore_wait(barrier, len(everyone))

    drains = []

    def spread_to(phase, devices, src, dst, size):
        for i, device in enumerate(devices):
            remote(src(i), dst, send_sem.at[phase], recv_sem.at[phase], device).start()
        drains.append((phase, size))

    def arrived(phase, size):
        remote(size, size, send_sem.at[phase], recv_sem.at[phase], sibling).wait_recv()

    t_size = t_buf.at[pl.ds(0, NT - 1)]
    c_size = c_buf.at[pl.ds(0, NZ - 1)]
    r_size = r_buf.at[pl.ds(0, NYC - 1)]
    spread_to(0, [at_t(p) for p in t_peers], lambda i: t_buf.at[t], t_buf.at[t], t_size)
    spread_to(1, [at_z(p) for p in z_peers], lambda i: c_buf.at[z], c_buf.at[z], c_size)
    spread_to(
        2,
        [at_yc(p) for p in yc_peers],
        lambda i: slices.at[lax.rem(yc_peers[i], 2), yc_peers[i] // 2],
        r_buf.at[yc],
        r_size,
    )

    arrived(1, c_size)
    counts = c_buf[0] + c_buf[1] + c_buf[2] + c_buf[3]
    arrived(0, t_size)
    summed = t_buf[0]
    for p in range(1, NT):
        summed = summed + t_buf[p]
    square_all = summed[96:97]
    rs_row = lax.rsqrt(square_all * (1.0 / D) + 1e-05)
    rs_col = jnp.sum(jnp.where(eye, rs_row, 0.0), axis=1, keepdims=True)
    adapter = (summed[0:32] * ROOT).astype(BF).astype(F32)
    spread = jnp.dot(adapter[:, 0:RANK], summed[32:96], precision=EXACT, preferred_element_type=F32)
    back = COEF * (summed[0:32] + COEF * spread - rs_col * pltpu.roll(summed[64:96], RANK, 1))
    low16 = low[0:16]
    extra = jnp.where(iota((1, SIZE), 1) < ROWS, rs_row, 0.0) + onehot + pltpu.roll(counts, 32, 1)
    late[0, 0:16, :] = jnp.where(low16, pltpu.roll(back[0:16], RANK, 1), back[16:32])
    late[1, 0:16, :] = jnp.where(low16, adapter[0:16], pltpu.roll(adapter[16:32], RANK, 1))
    late[0, 16:17, :] = extra
    late[1, 16:17, :] = extra
    l_size = l_buf.at[pl.ds(0, NYC - 1), pl.ds(0, 17)]
    spread_to(
        3,
        [at_yc(p) for p in yc_peers],
        lambda i: late.at[lax.rem(yc_peers[i], 2), pl.ds(0, 17)],
        l_buf.at[yc, pl.ds(0, 17)],
        l_size,
    )
    l_buf[yc, 0:17, :] = late[c, 0:17, :]

    serve = (summed[32:64] * rs_col * ROOT).astype(BF)
    drafted = jnp.dot(serve[:, 0:RANK], w_b[RANK:, :], preferred_element_type=F32)
    for g in range(GROUP):
        cols = slice(g * SIZE, (g + 1) * SIZE)
        hidden = (slices[1, g] * rs_col).astype(BF)
        hid_v[:, cols] = hidden
        dn_v[:, cols] = (hidden.astype(F32) + COEF * drafted[:, cols]).astype(BF)
    stores = [
        pltpu.make_async_copy(hid_v, hid_hbm, out_sem.at[0]),
        pltpu.make_async_copy(dn_v, dn_hbm, out_sem.at[1]),
    ]
    for store in stores:
        store.start()

    arrived(2, r_size)
    remote(r_buf, x_buf, send_sem.at[4], recv_sem.at[4], sibling).start()
    drains.append((4, r_buf))
    arrived(4, r_buf)
    arrived(3, l_size)

    packed = l_buf[:, 0:16, :].reshape(256, SIZE)
    tiles = l_buf[:, 16:24, :]
    tiles = jnp.where(iota((NYC, 8, SIZE), 1) == 0, tiles, 0.0)
    lane = iota((256, SIZE), 1)
    load_all = pltpu.roll(jnp.sum(jnp.sum(tiles, axis=0), axis=0, keepdims=True), 96, 1)
    load_all = jnp.where(iota((1, SIZE), 1) // 16 == 4, load_all, 0.0)
    own_row = (lane == (iota((256, SIZE), 0) // 16) * 8).astype(F32)
    extras = jnp.dot(own_row, tiles.reshape(SIZE, SIZE), precision=EXACT, preferred_element_type=F32)
    weight = 1.0 / (ROWS * jnp.sum(extras * load_all, axis=1, keepdims=True))

    @pl.when(c == 0)
    def _():
        left = (packed * weight).astype(BF)
        top_rows = r_buf[:, 0:16, :].reshape(256, SIZE).astype(BF)
        bottom_rows = r_buf[:, 16:32, :].reshape(256, SIZE).astype(BF)
        z_buf[z] = (dot_rows(left, top_rows)[0:RANK] + dot_rows(left, bottom_rows)[RANK:]) * ROOT

    @pl.when(c == 1)
    def _():
        left = packed.astype(BF)
        up = w_b[RANK:, pl.ds(pl.multiple_of(y * SIZE, SIZE), SIZE)]
        none = jnp.zeros_like(up)
        place = lax.rem(iota((256, SIZE), 0), 16)

        def half(h, up_half):
            rs = jnp.sum(jnp.where(lane == place + 16 * h, extras, 0.0), axis=1, keepdims=True)
            rows = slice(16 * h, 16 * h + 16)
            drafts = x_buf[:, rows, :].reshape(256, SIZE)
            gained = r_buf[:, rows, :].reshape(256, SIZE)
            lift = jnp.dot(left, up_half, preferred_element_type=F32)
            resid = (weight * (drafts + COEF * lift - rs * gained)).astype(BF)
            return dot_rows(left, resid)

        top_part = half(0, jnp.concatenate([up, none], axis=0))
        bottom_part = half(1, jnp.concatenate([none, up], axis=0))
        z_buf[z] = (top_part[0:RANK] + bottom_part[RANK:]) * COEF

    z_size = z_buf.at[pl.ds(0, NZ - 1)]
    spread_to(5, [at_z(p) for p in z_peers], lambda i: z_buf.at[z], z_buf.at[z], z_size)
    arrived(5, z_size)
    grad = z_buf[0] + z_buf[1] + z_buf[2] + z_buf[3]
    grads[c, y] = grad

    s_y[y] = jnp.sum(grad * grad, axis=0, keepdims=True)
    own_core = [at_yc(p * 2 + c) for p in y_peers]
    s_size = s_y.at[pl.ds(0, NY - 1)]
    spread_to(6, own_core, lambda i: s_y.at[y], s_y.at[y], s_size)
    mine = grads.at[c, y]
    for device in own_core:
        remote(mine, mine, send_sem.at[7], slice_sem.at[y], device).start()
    g_size = grads.at[0, pl.ds(0, NY - 1)]
    drains.append((7, g_size))
    remote(mine, mine, send_sem.at[8], recv_sem.at[8], sibling).start()
    arrived(6, s_size)
    part = s_y[0]
    for p in range(1, NY):
        part = part + s_y[p]
    place_t = t * 2 + c
    s_t[place_t] = part
    st_size = s_t.at[pl.ds(0, 2 * NT - 1)]
    spread_to(
        9,
        [at_t(p) for p in t_peers] + [(z * NYC + y * 2 + 1 - c, p) for p in t_peers] + [sibling],
        lambda i: s_t.at[place_t],
        s_t.at[place_t],
        st_size,
    )
    for p in reversed(y_peers):
        piece = grads.at[c, p]
        remote(piece, piece, send_sem.at[7], slice_sem.at[p], sibling).wait_recv()
        remote(piece, piece, send_sem.at[8], recv_sem.at[8], sibling).start()
    drains.append((8, grads.at[0]))
    arrived(9, st_size)
    whole = s_t[0]
    for p in range(1, 2 * NT):
        whole = whole + s_t[p]
    total_sq = jnp.sum(whole, axis=1, keepdims=True)
    step = 0.5 / jnp.sqrt(total_sq * (1.0 / (2.0 * RANK * D)) + 1e-06)
    arrived(8, grads.at[0])
    for p in range(NY):
        cols = slice(p * SIZE, (p + 1) * SIZE)
        nd_v[:, cols] = fd_v[:, cols] - grads[0, p] * step
        nu_v[:, cols] = fu_v[:, cols] - grads[1, p] * step
    stores += [
        pltpu.make_async_copy(nd_v, nd_hbm, out_sem.at[2]),
        pltpu.make_async_copy(nu_v, nu_hbm, out_sem.at[3]),
    ]
    for store in stores[2:]:
        store.start()
    for phase, size in drains:
        remote(size, size, send_sem.at[phase], recv_sem.at[phase], sibling).wait_send()
    for store in stores:
        store.wait()


def hand_over(*refs):
    *refs, sem = refs
    copies = [pltpu.make_async_copy(refs[i], refs[4 + i], sem.at[i]) for i in (2, 3, 0, 1)]
    for copy in copies:
        copy.start()
    for copy in copies:
        copy.wait()


def local(
    queries,
    cache_keys,
    cache_values,
    new_keys,
    new_values,
    cache_lengths,
    residual,
    norm_gain,
    draft_input,
    trainer_of,
    factor_down,
    factor_up,
):
    inputs = (
        queries,
        cache_keys.reshape(ROWS, SIZE, SIZE),
        cache_values.reshape(ROWS, SIZE, SIZE),
        new_keys,
        new_values,
        cache_lengths.reshape(1, ROWS),
        residual,
        norm_gain.reshape(1, WIDTH),
        draft_input,
        trainer_of.reshape(1, 1),
        factor_down,
        factor_up,
    )
    outs = (
        jax.ShapeDtypeStruct((ROWS, WIDTH), BF),
        jax.ShapeDtypeStruct((ROWS, WIDTH), BF),
        jax.ShapeDtypeStruct((RANK, WIDTH), F32),
        jax.ShapeDtypeStruct((RANK, WIDTH), F32),
    )
    vmem = pltpu.VMEM
    dma = pltpu.SemaphoreType.DMA
    scratch = (
        [vmem(a.shape, a.dtype) for a in inputs]
        + [vmem(a.shape, a.dtype) for a in outs]
        + [
            vmem((2 * RANK, WIDTH), BF),
            vmem((ROWS * GROUP, SIZE), F32),
            vmem((ROWS * GROUP, SIZE), F32),
            vmem((ROWS, WIDTH), BF),
            vmem((2, NY, ROWS, SIZE), F32),
            vmem((NT, 104, SIZE), F32),
            vmem((NYC, ROWS, SIZE), F32),
            vmem((NYC, ROWS, SIZE), F32),
            vmem((2, 24, SIZE), F32),
            vmem((NYC, 24, SIZE), F32),
            vmem((NZ, 1, SIZE), F32),
            vmem((NZ, RANK, SIZE), F32),
            vmem((2, NY, RANK, SIZE), F32),
            vmem((2 * NT, 1, SIZE), F32),
            vmem((NY, 1, SIZE), F32),
            dma((len(inputs),)),
            dma((len(outs),)),
            dma((10,)),
            dma((10,)),
            dma((NY,)),
        ]
    )
    anywhere = pl.BlockSpec(memory_space=pl.ANY)
    results = pl.pallas_call(
        kernel,
        out_shape=outs,
        in_specs=[anywhere] * len(inputs),
        out_specs=tuple([anywhere] * len(outs)),
        scratch_shapes=scratch,
        compiler_params=pltpu.CompilerParams(
            collective_id=0, has_side_effects=True, vmem_limit_bytes=60 * 1024 * 1024
        ),
        name="decode_and_draft",
    )(*inputs)
    return tuple(
        pl.pallas_call(
            hand_over,
            out_shape=outs,
            in_specs=[anywhere] * len(outs),
            out_specs=tuple([anywhere] * len(outs)),
            scratch_shapes=[dma((len(outs),))],
            compiler_params=pltpu.CompilerParams(vmem_limit_bytes=60 * 1024 * 1024),
            name="hand_over",
        )(*results)
    )


def solution(mesh):
    return jax.shard_map(
        local,
        mesh=mesh,
        in_specs=(
            P("replica", "tensor"),
            P("replica", "tensor", None, None),
            P("replica", "tensor", None, None),
            P("replica", "tensor"),
            P("replica", "tensor"),
            P("replica"),
            P("replica", "tensor"),
            P("tensor"),
            P("replica", "tensor"),
            P("replica"),
            P(None, "tensor"),
            P(None, "tensor"),
        ),
        out_specs=(
            P("replica", "tensor"),
            P("replica", "tensor"),
            P(None, "tensor"),
            P(None, "tensor"),
        ),
        check_vma=False,
    )
```

```python
import functools
import math

import jax
import jax.numpy as jnp
from jax import lax
from jax.experimental import pallas as pl
from jax.experimental.pallas import tpu as pltpu
from jax.sharding import PartitionSpec as P

D = 8192
RANK = 64
ROWS = 32
GROUP = 8
SIZE = 128
WIDTH = 1024
NT = 8
NY = 8
NZ = 4
NYC = 16
ROOT = 1.0 / math.sqrt(D)
COEF = 0.5 / math.sqrt(RANK)
MESH = pl.DeviceIdType.MESH
BF = jnp.bfloat16
F32 = jnp.float32
EXACT = lax.Precision.HIGHEST


def iota(shape, dim):
    return lax.broadcasted_iota(jnp.int32, shape, dim)


def dot_t(a, b):
    return lax.dot_general(a, b, (((1,), (1,)), ((), ())), preferred_element_type=F32)


def dot_rows(a, b):
    return lax.dot_general(a, b, (((0,), (0,)), ((), ())), preferred_element_type=F32)


def remote(src, dst, send_sem, recv_sem, device):
    return pltpu.make_async_remote_copy(
        src_ref=src,
        dst_ref=dst,
        send_sem=send_sem,
        recv_sem=recv_sem,
        device_id=device,
        device_id_type=MESH,
    )


def kernel(
    q_hbm, ck_hbm, cv_hbm, nk_hbm, nv_hbm, len_hbm, res_hbm, gain_hbm, dr_hbm, tr_hbm, fd_hbm, fu_hbm,
    hid_v, dn_v, nd_v, nu_v,
    q_v, ck_v, cv_v, nk_v, nv_v, len_v, res_v, gain_v, dr_v, tr_v, fd_v, fu_v,
    w_b, q3, ctx3, fg_b,
    slices, t_buf, r_buf, x_buf, late, l_buf, c_buf, z_buf, grads, s_t, s_y,
    in_sem, send_sem, recv_sem, slice_sem,
):
    r = lax.axis_index("replica")
    t = lax.axis_index("tensor")
    yc = lax.rem(r, NYC)
    z = r // NYC
    y = yc // 2
    c = lax.rem(yc, 2)
    x = t // 2
    low_z = lax.rem(t, 2)
    y_order = (4, 3, 5, 2, 6, 1, 7)
    t_peers = [
        lax.rem(x + dx, 4) * 2 + lax.rem(low_z + dz, 2)
        for dx, dz in ((2, 1), (1, 1), (3, 1), (2, 0), (1, 0), (3, 0), (0, 1))
    ]
    yc_peers = [lax.rem(y + dy, NY) * 2 + lax.rem(c + dc, 2) for dy in y_order for dc in (0, 1)]
    yc_peers = yc_peers + [y * 2 + 1 - c]
    z_peers = [lax.rem(z + dz, NZ) for dz in (2, 1, 3)]
    y_peers = [lax.rem(y + dy, NY) for dy in y_order]

    def at_t(p):
        return (r, p)

    def at_yc(p):
        return (z * NYC + p, t)

    def at_z(p):
        return (p * NYC + yc, t)

    sibling = at_yc(y * 2 + 1 - c)

    barrier = pltpu.get_barrier_semaphore()
    everyone = (
        [at_t(p) for p in t_peers]
        + [at_yc(p) for p in yc_peers]
        + [at_z(p) for p in z_peers]
        + [(z * NYC + y * 2 + 1 - c, p) for p in t_peers]
    )
    for device in everyone:
        pl.semaphore_signal(barrier, inc=1, device_id=device, device_id_type=MESH)

    loads = [
        pltpu.make_async_copy(src, dst, in_sem.at[i])
        for i, (src, dst) in enumerate(
            (
                (fd_hbm, fd_v), (fu_hbm, fu_v), (dr_hbm, dr_v), (q_hbm, q_v), (nk_hbm, nk_v), (len_hbm, len_v),
                (ck_hbm, ck_v), (nv_hbm, nv_v), (res_hbm, res_v), (gain_hbm, gain_v), (tr_hbm, tr_v), (cv_hbm, cv_v),
            )
        )
    ]
    for load in loads:
        load.start()
    for load in loads[:3]:
        load.wait()

    w_b[0:RANK, :] = fd_v[...].astype(BF)
    w_b[RANK:, :] = fu_v[...].astype(BF)
    draft_part = dot_t(dr_v[...], w_b[...])
    up_part = dot_t(w_b[RANK:, :], w_b[...])
    for g in range(GROUP):
        slices[0, g] = dr_v[:, g * SIZE : (g + 1) * SIZE].astype(F32)

    for load in loads[3:6]:
        load.wait()
    for g in range(GROUP):
        q3[pl.ds(g, ROWS, stride=GROUP), :] = q_v[:, g * SIZE : (g + 1) * SIZE].astype(F32)
    pick = (iota((ROWS * GROUP, ROWS), 0) // GROUP == iota((ROWS * GROUP, ROWS), 1)).astype(F32)
    own_key = jnp.dot(pick.astype(BF), nk_v[...], preferred_element_type=F32)
    lengths = jnp.dot(
        (pick * len_v[...].astype(F32)).astype(BF), jnp.ones((ROWS, SIZE), BF), preferred_element_type=F32
    )
    queries = q3[...]
    scale = 1.0 / math.sqrt(SIZE)
    own_score = jnp.sum(queries * own_key, axis=1, keepdims=True) * scale
    loads[6].wait()
    scores = lax.dot_general(
        queries.reshape(ROWS, GROUP, SIZE).astype(BF),
        ck_v[...],
        (((2,), (2,)), ((0,), (0,))),
        preferred_element_type=F32,
    ).reshape(ROWS * GROUP, SIZE)
    live = iota((ROWS * GROUP, SIZE), 1).astype(F32) < lengths
    scores = jnp.where(live, scores * scale, -jnp.inf)
    top = jnp.maximum(jnp.max(scores, axis=1, keepdims=True), own_score)
    weights = jnp.exp(scores - top)
    own_weight = jnp.exp(own_score - top)
    total = jnp.sum(weights, axis=1, keepdims=True) + own_weight
    probs = (weights / total).astype(BF)
    own_prob = (own_weight / total).astype(BF).astype(F32)
    for load in loads[7:]:
        load.wait()
    own_value = jnp.dot(pick.astype(BF), nv_v[...], preferred_element_type=F32)
    context = lax.dot_general(
        probs.reshape(ROWS, GROUP, SIZE),
        cv_v[...],
        (((2,), (1,)), ((0,), (0,))),
        preferred_element_type=F32,
    ).reshape(ROWS * GROUP, SIZE)
    ctx3[...] = context + own_prob * own_value

    squares = jnp.zeros((ROWS, SIZE), F32)
    for g in range(GROUP):
        cols = slice(g * SIZE, (g + 1) * SIZE)
        feature = res_v[:, cols].astype(F32) + ctx3[pl.ds(g, ROWS, stride=GROUP), :]
        squares = squares + feature * feature
        gained = feature * gain_v[:, cols]
        slices[1, g] = gained
        fg_b[:, cols] = gained.astype(BF)
    square_col = jnp.sum(squares, axis=1, keepdims=True)
    eye = iota((ROWS, SIZE), 0) == iota((ROWS, SIZE), 1)
    square_row = jnp.sum(jnp.where(eye, square_col, 0.0), axis=0, keepdims=True)
    feature_part = dot_t(fg_b[...], w_b[...])
    low = iota((ROWS, SIZE), 1) < RANK

    t_buf[t, 0:32, :] = draft_part
    t_buf[t, 32:64, :] = jnp.where(low, feature_part, up_part[0:32])
    t_buf[t, 64:96, :] = jnp.where(low, pltpu.roll(feature_part, RANK, 1), up_part[32:64])
    t_buf[t, 96:104, :] = jnp.broadcast_to(square_row, (8, SIZE))
    onehot = (iota((1, SIZE), 1) == tr_v[...] + 64).astype(F32)
    c_buf[z] = onehot
    r_buf[yc] = slices[c, y]

    pl.semaphore_wait(barrier, len(everyone))

    drains = []

    def spread_to(phase, devices, src, dst, size):
        for i, device in enumerate(devices):
            remote(src(i), dst, send_sem.at[phase], recv_sem.at[phase], device).start()
        drains.append((phase, size))

    def arrived(phase, size):
        remote(size, size, send_sem.at[phase], recv_sem.at[phase], sibling).wait_recv()

    t_size = t_buf.at[pl.ds(0, NT - 1)]
    c_size = c_buf.at[pl.ds(0, NZ - 1)]
    r_size = r_buf.at[pl.ds(0, NYC - 1)]
    spread_to(0, [at_t(p) for p in t_peers], lambda i: t_buf.at[t], t_buf.at[t], t_size)
    spread_to(1, [at_z(p) for p in z_peers], lambda i: c_buf.at[z], c_buf.at[z], c_size)
    spread_to(
        2,
        [at_yc(p) for p in yc_peers],
        lambda i: slices.at[lax.rem(yc_peers[i], 2), yc_peers[i] // 2],
        r_buf.at[yc],
        r_size,
    )

    arrived(1, c_size)
    counts = c_buf[0] + c_buf[1] + c_buf[2] + c_buf[3]
    arrived(0, t_size)
    summed = t_buf[0]
    for p in range(1, NT):
        summed = summed + t_buf[p]
    square_all = summed[96:97]
    rs_row = lax.rsqrt(square_all * (1.0 / D) + 1e-05)
    rs_col = jnp.sum(jnp.where(eye, rs_row, 0.0), axis=1, keepdims=True)
    adapter = (summed[0:32] * ROOT).astype(BF).astype(F32)
    spread = jnp.dot(adapter[:, 0:RANK], summed[32:96], precision=EXACT, preferred_element_type=F32)
    back = COEF * (summed[0:32] + COEF * spread - rs_col * pltpu.roll(summed[64:96], RANK, 1))
    low16 = low[0:16]
    extra = jnp.where(iota((1, SIZE), 1) < ROWS, rs_row, 0.0) + onehot + pltpu.roll(counts, 32, 1)
    late[0, 0:16, :] = jnp.where(low16, pltpu.roll(back[0:16], RANK, 1), back[16:32])
    late[1, 0:16, :] = jnp.where(low16, adapter[0:16], pltpu.roll(adapter[16:32], RANK, 1))
    late[0, 16:17, :] = extra
    late[1, 16:17, :] = extra
    l_size = l_buf.at[pl.ds(0, NYC - 1), pl.ds(0, 17)]
    spread_to(
        3,
        [at_yc(p) for p in yc_peers],
        lambda i: late.at[lax.rem(yc_peers[i], 2), pl.ds(0, 17)],
        l_buf.at[yc, pl.ds(0, 17)],
        l_size,
    )
    l_buf[yc, 0:17, :] = late[c, 0:17, :]

    serve = (summed[32:64] * rs_col * ROOT).astype(BF)
    drafted = jnp.dot(serve[:, 0:RANK], w_b[RANK:, :], preferred_element_type=F32)
    for g in range(GROUP):
        cols = slice(g * SIZE, (g + 1) * SIZE)
        hidden = (slices[1, g] * rs_col).astype(BF)
        hid_v[:, cols] = hidden
        dn_v[:, cols] = (hidden.astype(F32) + COEF * drafted[:, cols]).astype(BF)

    arrived(2, r_size)
    remote(r_buf, x_buf, send_sem.at[4], recv_sem.at[4], sibling).start()
    drains.append((4, r_buf))
    arrived(4, r_buf)
    arrived(3, l_size)

    packed = l_buf[:, 0:16, :].reshape(256, SIZE)
    tiles = l_buf[:, 16:24, :]
    tiles = jnp.where(iota((NYC, 8, SIZE), 1) == 0, tiles, 0.0)
    lane = iota((256, SIZE), 1)
    load_all = pltpu.roll(jnp.sum(jnp.sum(tiles, axis=0), axis=0, keepdims=True), 96, 1)
    load_all = jnp.where(iota((1, SIZE), 1) // 16 == 4, load_all, 0.0)
    own_row = (lane == (iota((256, SIZE), 0) // 16) * 8).astype(F32)
    extras = jnp.dot(own_row, tiles.reshape(SIZE, SIZE), precision=EXACT, preferred_element_type=F32)
    weight = 1.0 / (ROWS * jnp.sum(extras * load_all, axis=1, keepdims=True))

    @pl.when(c == 0)
    def _():
        left = (packed * weight).astype(BF)
        top_rows = r_buf[:, 0:16, :].reshape(256, SIZE).astype(BF)
        bottom_rows = r_buf[:, 16:32, :].reshape(256, SIZE).astype(BF)
        z_buf[z] = (dot_rows(left, top_rows)[0:RANK] + dot_rows(left, bottom_rows)[RANK:]) * ROOT

    @pl.when(c == 1)
    def _():
        left = packed.astype(BF)
        up = w_b[RANK:, pl.ds(pl.multiple_of(y * SIZE, SIZE), SIZE)]
        none = jnp.zeros_like(up)
        place = lax.rem(iota((256, SIZE), 0), 16)

        def half(h, up_half):
            rs = jnp.sum(jnp.where(lane == place + 16 * h, extras, 0.0), axis=1, keepdims=True)
            rows = slice(16 * h, 16 * h + 16)
            drafts = x_buf[:, rows, :].reshape(256, SIZE)
            gained = r_buf[:, rows, :].reshape(256, SIZE)
            lift = jnp.dot(left, up_half, preferred_element_type=F32)
            resid = (weight * (drafts + COEF * lift - rs * gained)).astype(BF)
            return dot_rows(left, resid)

        top_part = half(0, jnp.concatenate([up, none], axis=0))
        bottom_part = half(1, jnp.concatenate([none, up], axis=0))
        z_buf[z] = (top_part[0:RANK] + bottom_part[RANK:]) * COEF

    z_size = z_buf.at[pl.ds(0, NZ - 1)]
    spread_to(5, [at_z(p) for p in z_peers], lambda i: z_buf.at[z], z_buf.at[z], z_size)
    arrived(5, z_size)
    grad = z_buf[0] + z_buf[1] + z_buf[2] + z_buf[3]
    grads[c, y] = grad

    s_y[y] = jnp.sum(grad * grad, axis=0, keepdims=True)
    own_core = [at_yc(p * 2 + c) for p in y_peers]
    s_size = s_y.at[pl.ds(0, NY - 1)]
    spread_to(6, own_core, lambda i: s_y.at[y], s_y.at[y], s_size)
    mine = grads.at[c, y]
    for device in own_core:
        remote(mine, mine, send_sem.at[7], slice_sem.at[y], device).start()
    g_size = grads.at[0, pl.ds(0, NY - 1)]
    drains.append((7, g_size))
    remote(mine, mine, send_sem.at[8], recv_sem.at[8], sibling).start()
    arrived(6, s_size)
    part = s_y[0]
    for p in range(1, NY):
        part = part + s_y[p]
    place_t = t * 2 + c
    s_t[place_t] = part
    st_size = s_t.at[pl.ds(0, 2 * NT - 1)]
    spread_to(
        9,
        [at_t(p) for p in t_peers] + [(z * NYC + y * 2 + 1 - c, p) for p in t_peers] + [sibling],
        lambda i: s_t.at[place_t],
        s_t.at[place_t],
        st_size,
    )
    for p in reversed(y_peers):
        piece = grads.at[c, p]
        remote(piece, piece, send_sem.at[7], slice_sem.at[p], sibling).wait_recv()
        remote(piece, piece, send_sem.at[8], recv_sem.at[8], sibling).start()
    drains.append((8, grads.at[0]))
    arrived(9, st_size)
    whole = s_t[0]
    for p in range(1, 2 * NT):
        whole = whole + s_t[p]
    total_sq = jnp.sum(whole, axis=1, keepdims=True)
    step = 0.5 / jnp.sqrt(total_sq * (1.0 / (2.0 * RANK * D)) + 1e-06)
    arrived(8, grads.at[0])
    for p in range(NY):
        cols = slice(p * SIZE, (p + 1) * SIZE)
        nd_v[:, cols] = fd_v[:, cols] - grads[0, p] * step
        nu_v[:, cols] = fu_v[:, cols] - grads[1, p] * step
    for phase, size in drains:
        remote(size, size, send_sem.at[phase], recv_sem.at[phase], sibling).wait_send()


def hand_over(*refs):
    *refs, sem = refs
    copies = [pltpu.make_async_copy(refs[i], refs[4 + i], sem.at[i]) for i in (2, 3, 0, 1)]
    for copy in copies:
        copy.start()
    for copy in copies:
        copy.wait()


def local(
    queries,
    cache_keys,
    cache_values,
    new_keys,
    new_values,
    cache_lengths,
    residual,
    norm_gain,
    draft_input,
    trainer_of,
    factor_down,
    factor_up,
):
    inputs = (
        queries,
        cache_keys.reshape(ROWS, SIZE, SIZE),
        cache_values.reshape(ROWS, SIZE, SIZE),
        new_keys,
        new_values,
        cache_lengths.reshape(1, ROWS),
        residual,
        norm_gain.reshape(1, WIDTH),
        draft_input,
        trainer_of.reshape(1, 1),
        factor_down,
        factor_up,
    )
    outs = (
        jax.ShapeDtypeStruct((ROWS, WIDTH), BF),
        jax.ShapeDtypeStruct((ROWS, WIDTH), BF),
        jax.ShapeDtypeStruct((RANK, WIDTH), F32),
        jax.ShapeDtypeStruct((RANK, WIDTH), F32),
    )
    vmem = pltpu.VMEM
    dma = pltpu.SemaphoreType.DMA
    scratch = (
        [vmem(a.shape, a.dtype) for a in inputs]
        + [
            vmem((2 * RANK, WIDTH), BF),
            vmem((ROWS * GROUP, SIZE), F32),
            vmem((ROWS * GROUP, SIZE), F32),
            vmem((ROWS, WIDTH), BF),
            vmem((2, NY, ROWS, SIZE), F32),
            vmem((NT, 104, SIZE), F32),
            vmem((NYC, ROWS, SIZE), F32),
            vmem((NYC, ROWS, SIZE), F32),
            vmem((2, 24, SIZE), F32),
            vmem((NYC, 24, SIZE), F32),
            vmem((NZ, 1, SIZE), F32),
            vmem((NZ, RANK, SIZE), F32),
            vmem((2, NY, RANK, SIZE), F32),
            vmem((2 * NT, 1, SIZE), F32),
            vmem((NY, 1, SIZE), F32),
            dma((len(inputs),)),
            dma((10,)),
            dma((10,)),
            dma((NY,)),
        ]
    )
    anywhere = pl.BlockSpec(memory_space=pl.ANY)
    results = pl.pallas_call(
        kernel,
        out_shape=tuple(vmem(a.shape, a.dtype) for a in outs),
        in_specs=[anywhere] * len(inputs),
        out_specs=tuple([pl.BlockSpec(memory_space=vmem)] * len(outs)),
        scratch_shapes=scratch,
        compiler_params=pltpu.CompilerParams(
            collective_id=0, has_side_effects=True, vmem_limit_bytes=60 * 1024 * 1024
        ),
        name="decode_and_draft",
    )(*inputs)
    return tuple(
        pl.pallas_call(
            hand_over,
            out_shape=outs,
            in_specs=[pl.BlockSpec(memory_space=vmem)] * len(outs),
            out_specs=tuple([anywhere] * len(outs)),
            scratch_shapes=[dma((len(outs),))],
            name="hand_over",
        )(*results)
    )


def solution(mesh):
    return jax.shard_map(
        local,
        mesh=mesh,
        in_specs=(
            P("replica", "tensor"),
            P("replica", "tensor", None, None),
            P("replica", "tensor", None, None),
            P("replica", "tensor"),
            P("replica", "tensor"),
            P("replica"),
            P("replica", "tensor"),
            P("tensor"),
            P("replica", "tensor"),
            P("replica"),
            P(None, "tensor"),
            P(None, "tensor"),
        ),
        out_specs=(
            P("replica", "tensor"),
            P("replica", "tensor"),
            P(None, "tensor"),
            P(None, "tensor"),
        ),
        check_vma=False,
    )
```

```python
import functools
import math

import jax
import jax.numpy as jnp
from jax import lax
from jax.experimental import pallas as pl
from jax.experimental.pallas import tpu as pltpu
from jax.sharding import PartitionSpec as P

D = 8192
RANK = 64
ROWS = 32
GROUP = 8
SIZE = 128
WIDTH = 1024
NT = 8
NY = 8
NZ = 4
NYC = 16
ROOT = 1.0 / math.sqrt(D)
COEF = 0.5 / math.sqrt(RANK)
MESH = pl.DeviceIdType.MESH
BF = jnp.bfloat16
F32 = jnp.float32
EXACT = lax.Precision.HIGHEST


def iota(shape, dim):
    return lax.broadcasted_iota(jnp.int32, shape, dim)


def dot_t(a, b):
    return lax.dot_general(a, b, (((1,), (1,)), ((), ())), preferred_element_type=F32)


def dot_rows(a, b):
    return lax.dot_general(a, b, (((0,), (0,)), ((), ())), preferred_element_type=F32)


def remote(src, dst, send_sem, recv_sem, device):
    return pltpu.make_async_remote_copy(
        src_ref=src,
        dst_ref=dst,
        send_sem=send_sem,
        recv_sem=recv_sem,
        device_id=device,
        device_id_type=MESH,
    )


def kernel(
    q_hbm, ck_hbm, cv_hbm, nk_hbm, nv_hbm, len_hbm, res_hbm, gain_hbm, dr_hbm, tr_hbm, fd_hbm, fu_hbm,
    hid_v, dn_v, nd_v, nu_v,
    q_v, ck_v, cv_v, nk_v, nv_v, len_v, res_v, gain_v, dr_v, tr_v, fd_v, fu_v,
    w_b, q3, ctx3, fg_b,
    slices, e_buf, f_buf, r_buf, x_buf, a_buf, l_buf, base, c_buf, z_buf, grads, s_t, s_y,
    in_sem, send_sem, recv_sem, slice_sem,
):
    r = lax.axis_index("replica")
    t = lax.axis_index("tensor")
    yc = lax.rem(r, NYC)
    z = r // NYC
    y = yc // 2
    c = lax.rem(yc, 2)
    x = t // 2
    low_z = lax.rem(t, 2)
    y_order = (4, 3, 5, 2, 6, 1, 7)
    t_peers = [
        lax.rem(x + dx, 4) * 2 + lax.rem(low_z + dz, 2)
        for dx, dz in ((2, 1), (1, 1), (3, 1), (2, 0), (1, 0), (3, 0), (0, 1))
    ]
    yc_peers = [lax.rem(y + dy, NY) * 2 + lax.rem(c + dc, 2) for dy in y_order for dc in (0, 1)]
    yc_peers = yc_peers + [y * 2 + 1 - c]
    z_peers = [lax.rem(z + dz, NZ) for dz in (2, 1, 3)]
    y_peers = [lax.rem(y + dy, NY) for dy in y_order]

    def at_t(p):
        return (r, p)

    def at_yc(p):
        return (z * NYC + p, t)

    def at_z(p):
        return (p * NYC + yc, t)

    sibling = at_yc(y * 2 + 1 - c)

    barrier = pltpu.get_barrier_semaphore()
    everyone = (
        [at_t(p) for p in t_peers]
        + [at_yc(p) for p in yc_peers]
        + [at_z(p) for p in z_peers]
        + [(z * NYC + y * 2 + 1 - c, p) for p in t_peers]
    )
    for device in everyone:
        pl.semaphore_signal(barrier, inc=1, device_id=device, device_id_type=MESH)

    loads = [
        pltpu.make_async_copy(src, dst, in_sem.at[i])
        for i, (src, dst) in enumerate(
            (
                (q_hbm, q_v), (nk_hbm, nk_v), (len_hbm, len_v), (tr_hbm, tr_v), (ck_hbm, ck_v), (fd_hbm, fd_v),
                (fu_hbm, fu_v), (dr_hbm, dr_v), (cv_hbm, cv_v), (nv_hbm, nv_v), (res_hbm, res_v), (gain_hbm, gain_v),
            )
        )
    ]
    for load in loads:
        load.start()
    for load in loads[:4]:
        load.wait()
    for g in range(GROUP):
        q3[pl.ds(g, ROWS, stride=GROUP), :] = q_v[:, g * SIZE : (g + 1) * SIZE].astype(F32)
    pick = (iota((ROWS * GROUP, ROWS), 0) // GROUP == iota((ROWS * GROUP, ROWS), 1)).astype(F32)
    own_key = jnp.dot(pick.astype(BF), nk_v[...], preferred_element_type=F32)
    lengths = jnp.dot(
        (pick * len_v[...].astype(F32)).astype(BF), jnp.ones((ROWS, SIZE), BF), preferred_element_type=F32
    )
    queries = q3[...]
    scale = 1.0 / math.sqrt(SIZE)
    own_score = jnp.sum(queries * own_key, axis=1, keepdims=True) * scale
    loads[4].wait()
    scores = lax.dot_general(
        queries.reshape(ROWS, GROUP, SIZE).astype(BF),
        ck_v[...],
        (((2,), (2,)), ((0,), (0,))),
        preferred_element_type=F32,
    ).reshape(ROWS * GROUP, SIZE)

    for load in loads[5:8]:
        load.wait()
    low = iota((ROWS, SIZE), 1) < RANK
    w_b[0:RANK, :] = fd_v[...].astype(BF)
    w_b[RANK:, :] = fu_v[...].astype(BF)
    for g in range(GROUP):
        slices[0, g] = dr_v[:, g * SIZE : (g + 1) * SIZE].astype(F32)
    e_buf[t, 0:32, :] = dot_t(dr_v[...], w_b[...])
    up_part = dot_t(w_b[RANK:, :], w_b[...])
    e_buf[t, 32:64, :] = jnp.where(low, pltpu.roll(up_part[0:32], RANK, 1), up_part[32:64])
    onehot = (iota((1, SIZE), 1) == tr_v[...] + 64).astype(F32)
    c_buf[z] = onehot

    live = iota((ROWS * GROUP, SIZE), 1).astype(F32) < lengths
    scores = jnp.where(live, scores * scale, -jnp.inf)
    top = jnp.maximum(jnp.max(scores, axis=1, keepdims=True), own_score)
    weights = jnp.exp(scores - top)
    own_weight = jnp.exp(own_score - top)
    total = jnp.sum(weights, axis=1, keepdims=True) + own_weight
    probs = (weights / total).astype(BF)
    own_prob = (own_weight / total).astype(BF).astype(F32)

    pl.semaphore_wait(barrier, len(everyone))
    drains = []

    def start(phase, src, dst, device):
        remote(src, dst, send_sem.at[phase], recv_sem.at[phase], device).start()

    def spread_to(phase, devices, src, size):
        for device in devices:
            start(phase, src, src, device)
        drains.append((phase, size))

    def arrived(phase, size):
        remote(size, size, send_sem.at[phase], recv_sem.at[phase], sibling).wait_recv()

    e_size = e_buf.at[pl.ds(0, NT - 1)]
    f_size = f_buf.at[pl.ds(0, NT - 1), pl.ds(0, 33)]
    c_size = c_buf.at[pl.ds(0, NZ - 1)]
    r_size = r_buf.at[pl.ds(0, NYC - 1)]
    spread_to(0, [at_t(p) for p in t_peers], e_buf.at[t], e_size)
    spread_to(1, [at_z(p) for p in z_peers], c_buf.at[z], c_size)
    for p in y_peers:
        start(2, slices.at[0, p], r_buf.at[yc], at_yc(p * 2))

    for load in loads[8:]:
        load.wait()
    own_value = jnp.dot(pick.astype(BF), nv_v[...], preferred_element_type=F32)
    context = lax.dot_general(
        probs.reshape(ROWS, GROUP, SIZE),
        cv_v[...],
        (((2,), (1,)), ((0,), (0,))),
        preferred_element_type=F32,
    ).reshape(ROWS * GROUP, SIZE)
    ctx3[...] = context + own_prob * own_value

    squares = jnp.zeros((ROWS, SIZE), F32)
    for g in range(GROUP):
        cols = slice(g * SIZE, (g + 1) * SIZE)
        feature = res_v[:, cols].astype(F32) + ctx3[pl.ds(g, ROWS, stride=GROUP), :]
        squares = squares + feature * feature
        gained = feature * gain_v[:, cols]
        slices[1, g] = gained
        fg_b[:, cols] = gained.astype(BF)
    square_col = jnp.sum(squares, axis=1, keepdims=True)
    eye = iota((ROWS, SIZE), 0) == iota((ROWS, SIZE), 1)
    square_row = jnp.sum(jnp.where(eye, square_col, 0.0), axis=0, keepdims=True)
    feature_part = dot_t(fg_b[...], w_b[...])
    f_buf[t, 0:32, :] = feature_part
    f_buf[t, 32:33, :] = square_row
    spread_to(3, [at_t(p) for p in t_peers], f_buf.at[t, pl.ds(0, 33)], f_size)
    for p in y_peers:
        start(2, slices.at[1, p], r_buf.at[yc], at_yc(p * 2 + 1))
    start(2, slices.at[1 - c, y], r_buf.at[yc], sibling)
    drains.append((2, r_size))
    r_buf[yc] = slices[c, y]

    arrived(0, e_size)
    early = e_buf[0]
    for p in range(1, NT):
        early = early + e_buf[p]
    low16 = low[0:16]
    adapter = (early[0:32] * ROOT).astype(BF).astype(F32)
    a_buf[yc] = jnp.where(low16, adapter[0:16], pltpu.roll(adapter[16:32], RANK, 1))
    for p in y_peers:
        start(4, a_buf.at[yc], a_buf.at[yc], at_yc(p * 2 + 1))
    start(4, a_buf.at[yc], a_buf.at[yc], sibling)
    drains.append((4, a_buf.at[pl.ds(0, NY)]))
    ups = early[32:64]
    upper = jnp.dot(adapter[:, 0:32], ups, precision=EXACT, preferred_element_type=F32)
    lower = jnp.dot(pltpu.roll(adapter, 96, 1)[:, 0:32], ups, precision=EXACT, preferred_element_type=F32)
    ahead = early[0:32] + COEF * (pltpu.roll(upper, RANK, 1) + lower)
    arrived(1, c_size)
    counts = c_buf[0] + c_buf[1] + c_buf[2] + c_buf[3]
    marks = onehot + pltpu.roll(counts, 32, 1)
    arrived(3, f_size)
    summed = f_buf[0, 0:33, :]
    for p in range(1, NT):
        summed = summed + f_buf[p, 0:33, :]
    rs_row = lax.rsqrt(summed[32:33] * (1.0 / D) + 1e-05)
    rs_col = jnp.sum(jnp.where(eye, rs_row, 0.0), axis=1, keepdims=True)
    back = COEF * (ahead - rs_col * summed[0:32])
    l_buf[yc, 0:16, :] = jnp.where(low16, pltpu.roll(back[0:16], RANK, 1), back[16:32])
    l_buf[yc, 16:17, :] = jnp.where(iota((1, SIZE), 1) < ROWS, rs_row, 0.0) + marks
    l_mine = l_buf.at[yc, pl.ds(0, 17)]
    l_row = l_buf.at[yc, pl.ds(16, 1)]
    for p in y_peers:
        start(5, l_mine, l_mine, at_yc(p * 2))
        start(6, l_row, l_row, at_yc(p * 2 + 1))
    start(5, l_mine, l_mine, sibling)
    drains.append((5, l_buf.at[pl.ds(0, NY), pl.ds(0, 17)]))
    drains.append((6, l_buf.at[pl.ds(0, NY - 1), pl.ds(16, 1)]))

    arrived(2, r_size)

    @pl.when(c == 0)
    def _():
        start(7, r_buf, x_buf, sibling)

    serve = (summed[0:32] * rs_col * ROOT).astype(BF)
    drafted = jnp.dot(serve[:, 0:RANK], w_b[RANK:, :], preferred_element_type=F32)
    for g in range(GROUP):
        cols = slice(g * SIZE, (g + 1) * SIZE)
        hidden = (slices[1, g] * rs_col).astype(BF)
        hid_v[:, cols] = hidden
        dn_v[:, cols] = (hidden.astype(F32) + COEF * drafted[:, cols]).astype(BF)

    @pl.when(c == 0)
    def _():
        arrived(4, a_buf.at[0])
        arrived(5, l_buf.at[pl.ds(0, NYC - 1), pl.ds(0, 17)])

    @pl.when(c == 1)
    def _():
        arrived(4, a_buf.at[pl.ds(0, NYC - 1)])
        left = a_buf[...].reshape(256, SIZE).astype(BF)
        up = w_b[RANK:, pl.ds(pl.multiple_of(y * SIZE, SIZE), SIZE)]
        none = jnp.zeros_like(up)
        lift_top = jnp.dot(left, jnp.concatenate([up, none], axis=0), preferred_element_type=F32)
        lift_bottom = jnp.dot(left, jnp.concatenate([none, up], axis=0), preferred_element_type=F32)
        arrived(7, x_buf)
        base[0] = x_buf[:, 0:16, :].reshape(256, SIZE) + COEF * lift_top
        base[1] = x_buf[:, 16:32, :].reshape(256, SIZE) + COEF * lift_bottom
        arrived(5, l_buf.at[0, pl.ds(0, 17)])
        arrived(6, l_buf.at[pl.ds(0, NYC - 2), pl.ds(16, 1)])

    tiles = l_buf[:, 16:24, :]
    tiles = jnp.where(iota((NYC, 8, SIZE), 1) == 0, tiles, 0.0)
    lane = iota((256, SIZE), 1)
    load_all = pltpu.roll(jnp.sum(jnp.sum(tiles, axis=0), axis=0, keepdims=True), 96, 1)
    load_all = jnp.where(iota((1, SIZE), 1) // 16 == 4, load_all, 0.0)
    own_row = (lane == (iota((256, SIZE), 0) // 16) * 8).astype(F32)
    extras = jnp.dot(own_row, tiles.reshape(SIZE, SIZE), precision=EXACT, preferred_element_type=F32)
    weight = 1.0 / (ROWS * jnp.sum(extras * load_all, axis=1, keepdims=True))

    @pl.when(c == 0)
    def _():
        left = (l_buf[:, 0:16, :].reshape(256, SIZE) * weight).astype(BF)
        top_rows = r_buf[:, 0:16, :].reshape(256, SIZE).astype(BF)
        bottom_rows = r_buf[:, 16:32, :].reshape(256, SIZE).astype(BF)
        z_buf[z] = (dot_rows(left, top_rows)[0:RANK] + dot_rows(left, bottom_rows)[RANK:]) * ROOT

    @pl.when(c == 1)
    def _():
        left = a_buf[...].reshape(256, SIZE).astype(BF)
        place = lax.rem(iota((256, SIZE), 0), 16)

        def half(h):
            rs = jnp.sum(jnp.where(lane == place + 16 * h, extras, 0.0), axis=1, keepdims=True)
            gained = r_buf[:, 16 * h : 16 * h + 16, :].reshape(256, SIZE)
            return dot_rows(left, (weight * (base[h] - rs * gained)).astype(BF))

        z_buf[z] = (half(0)[0:RANK] + half(1)[RANK:]) * COEF

    z_size = z_buf.at[pl.ds(0, NZ - 1)]
    spread_to(8, [at_z(p) for p in z_peers], z_buf.at[z], z_size)
    arrived(8, z_size)
    grad = z_buf[0] + z_buf[1] + z_buf[2] + z_buf[3]
    grads[c, y] = grad

    s_y[y] = jnp.sum(grad * grad, axis=0, keepdims=True)
    own_core = [at_yc(p * 2 + c) for p in y_peers]
    s_size = s_y.at[pl.ds(0, NY - 1)]
    spread_to(9, own_core, s_y.at[y], s_size)
    mine = grads.at[c, y]
    for device in own_core:
        remote(mine, mine, send_sem.at[10], slice_sem.at[y], device).start()
    g_size = grads.at[0, pl.ds(0, NY - 1)]
    drains.append((10, g_size))
    start(11, mine, mine, sibling)
    arrived(9, s_size)
    part = s_y[0]
    for p in range(1, NY):
        part = part + s_y[p]
    place_t = t * 2 + c
    s_t[place_t] = part
    st_size = s_t.at[pl.ds(0, 2 * NT - 1)]
    spread_to(
        12,
        [at_t(p) for p in t_peers] + [(z * NYC + y * 2 + 1 - c, p) for p in t_peers] + [sibling],
        s_t.at[place_t],
        st_size,
    )
    for p in reversed(y_peers):
        piece = grads.at[c, p]
        remote(piece, piece, send_sem.at[10], slice_sem.at[p], sibling).wait_recv()
        start(11, piece, piece, sibling)
    drains.append((11, grads.at[0]))
    arrived(12, st_size)
    whole = s_t[0]
    for p in range(1, 2 * NT):
        whole = whole + s_t[p]
    total_sq = jnp.sum(whole, axis=1, keepdims=True)
    step = 0.5 / jnp.sqrt(total_sq * (1.0 / (2.0 * RANK * D)) + 1e-06)
    arrived(11, grads.at[0])
    for p in range(NY):
        cols = slice(p * SIZE, (p + 1) * SIZE)
        nd_v[:, cols] = fd_v[:, cols] - grads[0, p] * step
        nu_v[:, cols] = fu_v[:, cols] - grads[1, p] * step
    for phase, size in drains:
        remote(size, size, send_sem.at[phase], recv_sem.at[phase], sibling).wait_send()

    @pl.when(c == 0)
    def _():
        remote(r_buf, x_buf, send_sem.at[7], recv_sem.at[7], sibling).wait_send()


def hand_over(*refs):
    *refs, sem = refs
    copies = [pltpu.make_async_copy(refs[i], refs[4 + i], sem.at[i]) for i in (2, 3, 0, 1)]
    for copy in copies:
        copy.start()
    for copy in copies:
        copy.wait()


def local(
    queries,
    cache_keys,
    cache_values,
    new_keys,
    new_values,
    cache_lengths,
    residual,
    norm_gain,
    draft_input,
    trainer_of,
    factor_down,
    factor_up,
):
    inputs = (
        queries,
        cache_keys.reshape(ROWS, SIZE, SIZE),
        cache_values.reshape(ROWS, SIZE, SIZE),
        new_keys,
        new_values,
        cache_lengths.reshape(1, ROWS),
        residual,
        norm_gain.reshape(1, WIDTH),
        draft_input,
        trainer_of.reshape(1, 1),
        factor_down,
        factor_up,
    )
    outs = (
        jax.ShapeDtypeStruct((ROWS, WIDTH), BF),
        jax.ShapeDtypeStruct((ROWS, WIDTH), BF),
        jax.ShapeDtypeStruct((RANK, WIDTH), F32),
        jax.ShapeDtypeStruct((RANK, WIDTH), F32),
    )
    vmem = pltpu.VMEM
    dma = pltpu.SemaphoreType.DMA
    scratch = (
        [vmem(a.shape, a.dtype) for a in inputs]
        + [
            vmem((2 * RANK, WIDTH), BF),
            vmem((ROWS * GROUP, SIZE), F32),
            vmem((ROWS * GROUP, SIZE), F32),
            vmem((ROWS, WIDTH), BF),
            vmem((2, NY, ROWS, SIZE), F32),
            vmem((NT, 64, SIZE), F32),
            vmem((NT, 40, SIZE), F32),
            vmem((NYC, ROWS, SIZE), F32),
            vmem((NYC, ROWS, SIZE), F32),
            vmem((NYC, 16, SIZE), F32),
            vmem((NYC, 24, SIZE), F32),
            vmem((2, 256, SIZE), F32),
            vmem((NZ, 1, SIZE), F32),
            vmem((NZ, RANK, SIZE), F32),
            vmem((2, NY, RANK, SIZE), F32),
            vmem((2 * NT, 1, SIZE), F32),
            vmem((NY, 1, SIZE), F32),
            dma((len(inputs),)),
            dma((13,)),
            dma((13,)),
            dma((NY,)),
        ]
    )
    anywhere = pl.BlockSpec(memory_space=pl.ANY)
    results = pl.pallas_call(
        kernel,
        out_shape=tuple(vmem(a.shape, a.dtype) for a in outs),
        in_specs=[anywhere] * len(inputs),
        out_specs=tuple([pl.BlockSpec(memory_space=vmem)] * len(outs)),
        scratch_shapes=scratch,
        compiler_params=pltpu.CompilerParams(
            collective_id=0, has_side_effects=True, vmem_limit_bytes=60 * 1024 * 1024
        ),
        name="decode_and_draft",
    )(*inputs)
    return tuple(
        pl.pallas_call(
            hand_over,
            out_shape=outs,
            in_specs=[pl.BlockSpec(memory_space=vmem)] * len(outs),
            out_specs=tuple([anywhere] * len(outs)),
            scratch_shapes=[dma((len(outs),))],
            compiler_params=pltpu.CompilerParams(vmem_limit_bytes=4 * 1024 * 1024),
            name="hand_over",
        )(*results)
    )


def solution(mesh):
    return jax.shard_map(
        local,
        mesh=mesh,
        in_specs=(
            P("replica", "tensor"),
            P("replica", "tensor", None, None),
            P("replica", "tensor", None, None),
            P("replica", "tensor"),
            P("replica", "tensor"),
            P("replica"),
            P("replica", "tensor"),
            P("tensor"),
            P("replica", "tensor"),
            P("replica"),
            P(None, "tensor"),
            P(None, "tensor"),
        ),
        out_specs=(
            P("replica", "tensor"),
            P("replica", "tensor"),
            P(None, "tensor"),
            P(None, "tensor"),
        ),
        check_vma=False,
    )
```

```python
import functools
import math

import jax
import jax.numpy as jnp
from jax import lax
from jax.experimental import pallas as pl
from jax.experimental.pallas import tpu as pltpu
from jax.sharding import PartitionSpec as P

D = 8192
RANK = 64
ROWS = 32
GROUP = 8
SIZE = 128
WIDTH = 1024
NT = 8
NY = 8
NZ = 4
NYC = 16
ROOT = 1.0 / math.sqrt(D)
COEF = 0.5 / math.sqrt(RANK)
MESH = pl.DeviceIdType.MESH
BF = jnp.bfloat16
F32 = jnp.float32
EXACT = lax.Precision.HIGHEST


def iota(shape, dim):
    return lax.broadcasted_iota(jnp.int32, shape, dim)


def dot_t(a, b):
    return lax.dot_general(a, b, (((1,), (1,)), ((), ())), preferred_element_type=F32)


def dot_rows(a, b):
    return lax.dot_general(a, b, (((0,), (0,)), ((), ())), preferred_element_type=F32)


def remote(src, dst, send_sem, recv_sem, device):
    return pltpu.make_async_remote_copy(
        src_ref=src,
        dst_ref=dst,
        send_sem=send_sem,
        recv_sem=recv_sem,
        device_id=device,
        device_id_type=MESH,
    )


def kernel(
    q_hbm, ck_hbm, cv_hbm, nk_hbm, nv_hbm, len_hbm, res_hbm, gain_hbm, dr_hbm, tr_hbm, fd_hbm, fu_hbm,
    hid_v, dn_v, nd_v, nu_v,
    q_v, ck_v, cv_v, nk_v, nv_v, len_v, res_v, gain_v, dr_v, tr_v, fd_v, fu_v,
    w_b, q3, ctx3, fg_b,
    slices, e_buf, u_buf, f_buf, h_buf, r_buf, x_buf, a_buf, l_buf, base, c_buf, z_buf, grads, s_t, s_y,
    in_sem, send_sem, recv_sem, slice_sem,
):
    r = lax.axis_index("replica")
    t = lax.axis_index("tensor")
    yc = lax.rem(r, NYC)
    z = r // NYC
    y = yc // 2
    c = lax.rem(yc, 2)
    x = t // 2
    low_z = lax.rem(t, 2)
    y_order = (4, 3, 5, 2, 6, 1, 7)
    t_peers = [
        lax.rem(x + dx, 4) * 2 + lax.rem(low_z + dz, 2)
        for dx, dz in ((2, 1), (1, 1), (3, 1), (2, 0), (1, 0), (3, 0), (0, 1))
    ]
    yc_peers = [lax.rem(y + dy, NY) * 2 + lax.rem(c + dc, 2) for dy in y_order for dc in (0, 1)]
    yc_peers = yc_peers + [y * 2 + 1 - c]
    z_peers = [lax.rem(z + dz, NZ) for dz in (2, 1, 3)]
    y_peers = [lax.rem(y + dy, NY) for dy in y_order]

    def at_t(p):
        return (r, p)

    def at_yc(p):
        return (z * NYC + p, t)

    def at_z(p):
        return (p * NYC + yc, t)

    sibling = at_yc(y * 2 + 1 - c)

    barrier = pltpu.get_barrier_semaphore()
    everyone = (
        [at_t(p) for p in t_peers]
        + [at_yc(p) for p in yc_peers]
        + [at_z(p) for p in z_peers]
        + [(z * NYC + y * 2 + 1 - c, p) for p in t_peers]
    )
    for device in everyone:
        pl.semaphore_signal(barrier, inc=1, device_id=device, device_id_type=MESH)

    loads = [
        pltpu.make_async_copy(src, dst, in_sem.at[i])
        for i, (src, dst) in enumerate(
            (
                (fd_hbm, fd_v), (fu_hbm, fu_v), (dr_hbm, dr_v), (q_hbm, q_v), (nk_hbm, nk_v), (len_hbm, len_v),
                (tr_hbm, tr_v), (ck_hbm, ck_v), (cv_hbm, cv_v), (nv_hbm, nv_v), (res_hbm, res_v), (gain_hbm, gain_v),
            )
        )
    ]
    for load in loads:
        load.start()
    for load in loads[:3]:
        load.wait()
    low = iota((ROWS, SIZE), 1) < RANK
    low16 = low[0:16]
    w_b[0:RANK, :] = fd_v[...].astype(BF)
    w_b[RANK:, :] = fu_v[...].astype(BF)
    for g in range(GROUP):
        slices[0, g] = dr_v[:, g * SIZE : (g + 1) * SIZE].astype(F32)
    e_buf[t, 0:32, :] = dot_t(dr_v[...], w_b[...])
    up_part = dot_t(w_b[RANK:, :], w_b[...])
    up_half = jnp.where(c == 0, up_part[0:32], up_part[32:64])
    e_buf[t, 32:48, :] = jnp.where(low16, pltpu.roll(up_half[0:16], RANK, 1), up_half[16:32])

    for load in loads[3:7]:
        load.wait()
    for g in range(GROUP):
        q3[pl.ds(g, ROWS, stride=GROUP), :] = q_v[:, g * SIZE : (g + 1) * SIZE].astype(F32)
    pick = (iota((ROWS * GROUP, ROWS), 0) // GROUP == iota((ROWS * GROUP, ROWS), 1)).astype(F32)
    own_key = jnp.dot(pick.astype(BF), nk_v[...], preferred_element_type=F32)
    lengths = jnp.dot(
        (pick * len_v[...].astype(F32)).astype(BF), jnp.ones((ROWS, SIZE), BF), preferred_element_type=F32
    )
    queries = q3[...]
    scale = 1.0 / math.sqrt(SIZE)
    own_score = jnp.sum(queries * own_key, axis=1, keepdims=True) * scale
    onehot = (iota((1, SIZE), 1) == tr_v[...] + 64).astype(F32)
    c_buf[z] = onehot
    loads[7].wait()
    scores = lax.dot_general(
        queries.reshape(ROWS, GROUP, SIZE).astype(BF),
        ck_v[...],
        (((2,), (2,)), ((0,), (0,))),
        preferred_element_type=F32,
    ).reshape(ROWS * GROUP, SIZE)

    pl.semaphore_wait(barrier, len(everyone))
    drains = []

    def start(phase, src, dst, device):
        remote(src, dst, send_sem.at[phase], recv_sem.at[phase], device).start()

    def spread_to(phase, devices, src, size):
        for device in devices:
            start(phase, src, src, device)
        drains.append((phase, size))

    def arrived(phase, size):
        remote(size, size, send_sem.at[phase], recv_sem.at[phase], sibling).wait_recv()

    e_size = e_buf.at[pl.ds(0, NT - 1)]
    f_size = f_buf.at[pl.ds(0, NT - 1), pl.ds(0, 17)]
    c_size = c_buf.at[pl.ds(0, NZ - 1)]
    r_size = r_buf.at[pl.ds(0, NYC - 1)]
    spread_to(0, [at_t(p) for p in t_peers], e_buf.at[t], e_size)
    for p in y_peers:
        start(2, slices.at[0, p], r_buf.at[yc], at_yc(p * 2))

    live = iota((ROWS * GROUP, SIZE), 1).astype(F32) < lengths
    scores = jnp.where(live, scores * scale, -jnp.inf)
    top = jnp.maximum(jnp.max(scores, axis=1, keepdims=True), own_score)
    weights = jnp.exp(scores - top)
    own_weight = jnp.exp(own_score - top)
    total = jnp.sum(weights, axis=1, keepdims=True) + own_weight
    probs = (weights / total).astype(BF)
    own_prob = (own_weight / total).astype(BF).astype(F32)

    for load in loads[8:]:
        load.wait()
    own_value = jnp.dot(pick.astype(BF), nv_v[...], preferred_element_type=F32)
    context = lax.dot_general(
        probs.reshape(ROWS, GROUP, SIZE),
        cv_v[...],
        (((2,), (1,)), ((0,), (0,))),
        preferred_element_type=F32,
    ).reshape(ROWS * GROUP, SIZE)
    ctx3[...] = context + own_prob * own_value

    squares = jnp.zeros((ROWS, SIZE), F32)
    for g in range(GROUP):
        cols = slice(g * SIZE, (g + 1) * SIZE)
        feature = res_v[:, cols].astype(F32) + ctx3[pl.ds(g, ROWS, stride=GROUP), :]
        squares = squares + feature * feature
        gained = feature * gain_v[:, cols]
        slices[1, g] = gained
        fg_b[:, cols] = gained.astype(BF)
    square_col = jnp.sum(squares, axis=1, keepdims=True)
    eye = iota((ROWS, SIZE), 0) == iota((ROWS, SIZE), 1)
    square_row = jnp.sum(jnp.where(eye, square_col, 0.0), axis=0, keepdims=True)
    feature_part = dot_t(fg_b[...], w_b[...])
    f_buf[t, 0:16, :] = jnp.where(low16, pltpu.roll(feature_part[0:16], RANK, 1), feature_part[16:32])
    f_buf[t, 16:17, :] = square_row
    h_buf[t] = jnp.where(low16, feature_part[0:16], pltpu.roll(feature_part[16:32], RANK, 1))
    spread_to(3, [at_t(p) for p in t_peers], f_buf.at[t, pl.ds(0, 17)], f_size)
    spread_to(1, [at_z(p) for p in z_peers], c_buf.at[z], c_size)
    for p in y_peers:
        start(2, slices.at[1, p], r_buf.at[yc], at_yc(p * 2 + 1))
    start(2, slices.at[1 - c, y], r_buf.at[yc], sibling)
    drains.append((2, r_size))
    r_buf[yc] = slices[c, y]

    arrived(0, e_size)
    u_buf[c] = sum((e_buf[p, 32:48, :] for p in range(1, NT)), e_buf[0, 32:48, :])
    spread_to(13, [sibling], u_buf.at[c], u_buf.at[0])
    early = sum((e_buf[p, 0:32, :] for p in range(1, NT)), e_buf[0, 0:32, :])
    adapter = (early * ROOT).astype(BF).astype(F32)
    a_buf[yc] = jnp.where(low16, adapter[0:16], pltpu.roll(adapter[16:32], RANK, 1))
    for p in y_peers:
        start(4, a_buf.at[yc], a_buf.at[yc], at_yc(p * 2 + 1))
    start(4, a_buf.at[yc], a_buf.at[yc], sibling)
    drains.append((4, a_buf.at[pl.ds(0, NY)]))
    arrived(13, u_buf.at[0])
    ups = jnp.concatenate([pltpu.roll(u_buf[0], RANK, 1), u_buf[0], pltpu.roll(u_buf[1], RANK, 1), u_buf[1]], axis=0)
    spread = jnp.dot(adapter[:, 0:RANK], ups, precision=EXACT, preferred_element_type=F32)
    ahead = early + COEF * spread
    ahead = jnp.where(low16, pltpu.roll(ahead[0:16], RANK, 1), ahead[16:32])
    arrived(1, c_size)
    counts = c_buf[0] + c_buf[1] + c_buf[2] + c_buf[3]
    marks = onehot + pltpu.roll(counts, 32, 1)
    arrived(3, f_size)
    summed = sum((f_buf[p, 0:17, :] for p in range(1, NT)), f_buf[0, 0:17, :])
    rs_row = lax.rsqrt(summed[16:17] * (1.0 / D) + 1e-05)
    rs_col = jnp.sum(jnp.where(eye, rs_row, 0.0), axis=1, keepdims=True)
    l_buf[yc, 0:16, :] = COEF * (ahead - jnp.where(low16, rs_col[0:16], rs_col[16:32]) * summed[0:16])
    l_buf[yc, 16:17, :] = jnp.where(iota((1, SIZE), 1) < ROWS, rs_row, 0.0) + marks
    l_mine = l_buf.at[yc, pl.ds(0, 17)]
    l_row = l_buf.at[yc, pl.ds(16, 1)]
    for p in y_peers:
        start(5, l_mine, l_mine, at_yc(p * 2))
        start(6, l_row, l_row, at_yc(p * 2 + 1))
    start(5, l_mine, l_mine, sibling)
    drains.append((5, l_buf.at[pl.ds(0, NY), pl.ds(0, 17)]))
    drains.append((6, l_buf.at[pl.ds(0, NY - 1), pl.ds(16, 1)]))

    arrived(2, r_size)

    @pl.when(c == 0)
    def _():
        start(7, r_buf, x_buf, sibling)

    spread_to(14, [at_t(p) for p in t_peers], h_buf.at[t], h_buf.at[pl.ds(0, NT - 1)])

    @pl.when(c == 0)
    def _():
        arrived(4, a_buf.at[0])
        arrived(5, l_buf.at[pl.ds(0, NYC - 1), pl.ds(0, 17)])

    @pl.when(c == 1)
    def _():
        arrived(4, a_buf.at[pl.ds(0, NYC - 1)])
        left = a_buf[...].reshape(256, SIZE).astype(BF)
        up = w_b[RANK:, pl.ds(pl.multiple_of(y * SIZE, SIZE), SIZE)]
        none = jnp.zeros_like(up)
        lift_top = jnp.dot(left, jnp.concatenate([up, none], axis=0), preferred_element_type=F32)
        lift_bottom = jnp.dot(left, jnp.concatenate([none, up], axis=0), preferred_element_type=F32)
        arrived(7, x_buf)
        base[0] = x_buf[:, 0:16, :].reshape(256, SIZE) + COEF * lift_top
        base[1] = x_buf[:, 16:32, :].reshape(256, SIZE) + COEF * lift_bottom
        arrived(5, l_buf.at[0, pl.ds(0, 17)])
        arrived(6, l_buf.at[pl.ds(0, NYC - 2), pl.ds(16, 1)])

    rows_of = jnp.broadcast_to(l_buf[:, 16:17, :], (NYC, 16, SIZE))
    lane = iota((NYC, 16, SIZE), 2)
    load_all = pltpu.roll(jnp.sum(l_buf[:, 16:17, :], axis=0), 96, 1)
    load_all = jnp.where(iota((1, SIZE), 1) // 16 == 4, load_all, 0.0)
    weight = 1.0 / (ROWS * jnp.sum(rows_of * load_all[None], axis=2, keepdims=True))

    @pl.when(c == 0)
    def _():
        left = (l_buf[:, 0:16, :] * weight).reshape(256, SIZE).astype(BF)
        top_rows = r_buf[:, 0:16, :].reshape(256, SIZE).astype(BF)
        bottom_rows = r_buf[:, 16:32, :].reshape(256, SIZE).astype(BF)
        z_buf[z] = (dot_rows(left, top_rows)[0:RANK] + dot_rows(left, bottom_rows)[RANK:]) * ROOT

    @pl.when(c == 1)
    def _():
        left = a_buf[...].reshape(256, SIZE).astype(BF)
        place = iota((NYC, 16, SIZE), 1)

        def half(h):
            rs = jnp.sum(jnp.where(lane == place + 16 * h, rows_of, 0.0), axis=2, keepdims=True)
            resid = weight * (base[h].reshape(NYC, 16, SIZE) - rs * r_buf[:, 16 * h : 16 * h + 16, :])
            return dot_rows(left, resid.reshape(256, SIZE).astype(BF))

        z_buf[z] = (half(0)[0:RANK] + half(1)[RANK:]) * COEF

    z_size = z_buf.at[pl.ds(0, NZ - 1)]
    spread_to(8, [at_z(p) for p in z_peers], z_buf.at[z], z_size)
    arrived(14, h_buf.at[pl.ds(0, NT - 1)])
    served = sum((h_buf[p] for p in range(1, NT)), h_buf[0])
    served = jnp.concatenate([served, pltpu.roll(served, RANK, 1)], axis=0)
    serve = (served * rs_col * ROOT).astype(BF)
    drafted = jnp.dot(serve[:, 0:RANK], w_b[RANK:, :], preferred_element_type=F32)
    for g in range(GROUP):
        cols = slice(g * SIZE, (g + 1) * SIZE)
        hidden = (slices[1, g] * rs_col).astype(BF)
        hid_v[:, cols] = hidden
        dn_v[:, cols] = (hidden.astype(F32) + COEF * drafted[:, cols]).astype(BF)

    arrived(8, z_size)
    grad = z_buf[0] + z_buf[1] + z_buf[2] + z_buf[3]
    grads[c, y] = grad

    s_y[y] = jnp.sum(grad * grad, axis=0, keepdims=True)
    own_core = [at_yc(p * 2 + c) for p in y_peers]
    s_size = s_y.at[pl.ds(0, NY - 1)]
    spread_to(9, own_core, s_y.at[y], s_size)
    mine = grads.at[c, y]
    for device in own_core:
        remote(mine, mine, send_sem.at[10], slice_sem.at[y], device).start()
    g_size = grads.at[0, pl.ds(0, NY - 1)]
    drains.append((10, g_size))
    start(11, mine, mine, sibling)
    arrived(9, s_size)
    part = s_y[0]
    for p in range(1, NY):
        part = part + s_y[p]
    place_t = t * 2 + c
    s_t[place_t] = part
    st_size = s_t.at[pl.ds(0, 2 * NT - 1)]
    spread_to(
        12,
        [at_t(p) for p in t_peers] + [(z * NYC + y * 2 + 1 - c, p) for p in t_peers] + [sibling],
        s_t.at[place_t],
        st_size,
    )
    for p in reversed(y_peers):
        piece = grads.at[c, p]
        remote(piece, piece, send_sem.at[10], slice_sem.at[p], sibling).wait_recv()
        start(11, piece, piece, sibling)
    drains.append((11, grads.at[0]))
    arrived(12, st_size)
    whole = s_t[0]
    for p in range(1, 2 * NT):
        whole = whole + s_t[p]
    total_sq = jnp.sum(whole, axis=1, keepdims=True)
    step = 0.5 / jnp.sqrt(total_sq * (1.0 / (2.0 * RANK * D)) + 1e-06)
    arrived(11, grads.at[0])
    for p in range(NY):
        cols = slice(p * SIZE, (p + 1) * SIZE)
        nd_v[:, cols] = fd_v[:, cols] - grads[0, p] * step
        nu_v[:, cols] = fu_v[:, cols] - grads[1, p] * step
    for phase, size in drains:
        remote(size, size, send_sem.at[phase], recv_sem.at[phase], sibling).wait_send()

    @pl.when(c == 0)
    def _():
        remote(r_buf, x_buf, send_sem.at[7], recv_sem.at[7], sibling).wait_send()


def hand_over(*refs):
    *refs, sem = refs
    copies = [pltpu.make_async_copy(refs[i], refs[4 + i], sem.at[i]) for i in (2, 3, 0, 1)]
    for copy in copies:
        copy.start()
    for copy in copies:
        copy.wait()


def local(
    queries,
    cache_keys,
    cache_values,
    new_keys,
    new_values,
    cache_lengths,
    residual,
    norm_gain,
    draft_input,
    trainer_of,
    factor_down,
    factor_up,
):
    inputs = (
        queries,
        cache_keys.reshape(ROWS, SIZE, SIZE),
        cache_values.reshape(ROWS, SIZE, SIZE),
        new_keys,
        new_values,
        cache_lengths.reshape(1, ROWS),
        residual,
        norm_gain.reshape(1, WIDTH),
        draft_input,
        trainer_of.reshape(1, 1),
        factor_down,
        factor_up,
    )
    outs = (
        jax.ShapeDtypeStruct((ROWS, WIDTH), BF),
        jax.ShapeDtypeStruct((ROWS, WIDTH), BF),
        jax.ShapeDtypeStruct((RANK, WIDTH), F32),
        jax.ShapeDtypeStruct((RANK, WIDTH), F32),
    )
    vmem = pltpu.VMEM
    dma = pltpu.SemaphoreType.DMA
    scratch = (
        [vmem(a.shape, a.dtype) for a in inputs]
        + [
            vmem((2 * RANK, WIDTH), BF),
            vmem((ROWS * GROUP, SIZE), F32),
            vmem((ROWS * GROUP, SIZE), F32),
            vmem((ROWS, WIDTH), BF),
            vmem((2, NY, ROWS, SIZE), F32),
            vmem((NT, 48, SIZE), F32),
            vmem((2, 16, SIZE), F32),
            vmem((NT, 24, SIZE), F32),
            vmem((NT, 16, SIZE), F32),
            vmem((NYC, ROWS, SIZE), F32),
            vmem((NYC, ROWS, SIZE), F32),
            vmem((NYC, 16, SIZE), F32),
            vmem((NYC, 24, SIZE), F32),
            vmem((2, 256, SIZE), F32),
            vmem((NZ, 1, SIZE), F32),
            vmem((NZ, RANK, SIZE), F32),
            vmem((2, NY, RANK, SIZE), F32),
            vmem((2 * NT, 1, SIZE), F32),
            vmem((NY, 1, SIZE), F32),
            dma((len(inputs),)),
            dma((15,)),
            dma((15,)),
            dma((NY,)),
        ]
    )
    anywhere = pl.BlockSpec(memory_space=pl.ANY)
    results = pl.pallas_call(
        kernel,
        out_shape=tuple(vmem(a.shape, a.dtype) for a in outs),
        in_specs=[anywhere] * len(inputs),
        out_specs=tuple([pl.BlockSpec(memory_space=vmem)] * len(outs)),
        scratch_shapes=scratch,
        compiler_params=pltpu.CompilerParams(
            collective_id=0, has_side_effects=True, vmem_limit_bytes=60 * 1024 * 1024
        ),
        name="decode_and_draft",
    )(*inputs)
    return tuple(
        pl.pallas_call(
            hand_over,
            out_shape=outs,
            in_specs=[pl.BlockSpec(memory_space=vmem)] * len(outs),
            out_specs=tuple([anywhere] * len(outs)),
            scratch_shapes=[dma((len(outs),))],
            compiler_params=pltpu.CompilerParams(vmem_limit_bytes=4 * 1024 * 1024),
            name="hand_over",
        )(*results)
    )


def solution(mesh):
    return jax.shard_map(
        local,
        mesh=mesh,
        in_specs=(
            P("replica", "tensor"),
            P("replica", "tensor", None, None),
            P("replica", "tensor", None, None),
            P("replica", "tensor"),
            P("replica", "tensor"),
            P("replica"),
            P("replica", "tensor"),
            P("tensor"),
            P("replica", "tensor"),
            P("replica"),
            P(None, "tensor"),
            P(None, "tensor"),
        ),
        out_specs=(
            P("replica", "tensor"),
            P("replica", "tensor"),
            P(None, "tensor"),
            P(None, "tensor"),
        ),
        check_vma=False,
    )
```

```python
import functools
import math

import jax
import jax.numpy as jnp
from jax import lax
from jax.experimental import pallas as pl
from jax.experimental.pallas import tpu as pltpu
from jax.sharding import PartitionSpec as P

D = 8192
RANK = 64
ROWS = 32
GROUP = 8
SIZE = 128
WIDTH = 1024
NT = 8
NY = 8
NZ = 4
NYC = 16
ROOT = 1.0 / math.sqrt(D)
COEF = 0.5 / math.sqrt(RANK)
MESH = pl.DeviceIdType.MESH
BF = jnp.bfloat16
F32 = jnp.float32
EXACT = lax.Precision.HIGHEST


def iota(shape, dim):
    return lax.broadcasted_iota(jnp.int32, shape, dim)


def dot_t(a, b):
    return lax.dot_general(a, b, (((1,), (1,)), ((), ())), preferred_element_type=F32)


def dot_rows(a, b):
    return lax.dot_general(a, b, (((0,), (0,)), ((), ())), preferred_element_type=F32)


def remote(src, dst, send_sem, recv_sem, device):
    return pltpu.make_async_remote_copy(
        src_ref=src,
        dst_ref=dst,
        send_sem=send_sem,
        recv_sem=recv_sem,
        device_id=device,
        device_id_type=MESH,
    )


def kernel(
    q_hbm, ck_hbm, cv_hbm, nk_hbm, nv_hbm, len_hbm, res_hbm, gain_hbm, dr_hbm, tr_hbm, fd_hbm, fu_hbm,
    hid_v, dn_v, nd_v, nu_v,
    q_v, ck_v, cv_v, nk_v, nv_v, len_v, res_v, gain_v, dr_v, tr_v, fd_v, fu_v,
    w_b, q3, ctx3, fg_b,
    slices, e_buf, u_buf, f_buf, h_buf, r_buf, x_buf, a_buf, l_buf, base, c_buf, z_buf, grads, s_t, s_y,
    in_sem, send_sem, recv_sem, slice_sem,
):
    r = lax.axis_index("replica")
    t = lax.axis_index("tensor")
    yc = lax.rem(r, NYC)
    z = r // NYC
    y = yc // 2
    c = lax.rem(yc, 2)
    x = t // 2
    low_z = lax.rem(t, 2)
    y_order = (4, 3, 5, 2, 6, 1, 7)
    t_peers = [
        lax.rem(x + dx, 4) * 2 + lax.rem(low_z + dz, 2)
        for dx, dz in ((2, 1), (1, 1), (3, 1), (2, 0), (1, 0), (3, 0), (0, 1))
    ]
    yc_peers = [lax.rem(y + dy, NY) * 2 + lax.rem(c + dc, 2) for dy in y_order for dc in (0, 1)]
    yc_peers = yc_peers + [y * 2 + 1 - c]
    z_peers = [lax.rem(z + dz, NZ) for dz in (2, 1, 3)]
    y_peers = [lax.rem(y + dy, NY) for dy in y_order]

    def at_t(p):
        return (r, p)

    def at_yc(p):
        return (z * NYC + p, t)

    def at_z(p):
        return (p * NYC + yc, t)

    sibling = at_yc(y * 2 + 1 - c)

    barrier = pltpu.get_barrier_semaphore()
    everyone = (
        [at_t(p) for p in t_peers]
        + [at_yc(p) for p in yc_peers]
        + [at_z(p) for p in z_peers]
        + [(z * NYC + y * 2 + 1 - c, p) for p in t_peers]
    )
    for device in everyone:
        pl.semaphore_signal(barrier, inc=1, device_id=device, device_id_type=MESH)

    loads = [
        pltpu.make_async_copy(src, dst, in_sem.at[i])
        for i, (src, dst) in enumerate(
            (
                (fd_hbm, fd_v), (fu_hbm, fu_v), (dr_hbm, dr_v), (q_hbm, q_v), (nk_hbm, nk_v), (len_hbm, len_v),
                (tr_hbm, tr_v), (ck_hbm, ck_v), (cv_hbm, cv_v), (nv_hbm, nv_v), (res_hbm, res_v), (gain_hbm, gain_v),
            )
        )
    ]
    for load in loads:
        load.start()
    for load in loads[:3]:
        load.wait()
    low = iota((ROWS, SIZE), 1) < RANK
    low16 = low[0:16]
    w_b[0:RANK, :] = fd_v[...].astype(BF)
    w_b[RANK:, :] = fu_v[...].astype(BF)
    for g in range(GROUP):
        slices[0, g] = dr_v[:, g * SIZE : (g + 1) * SIZE].astype(F32)
    e_buf[t, 0:32, :] = dot_t(dr_v[...], w_b[...])
    up_part = dot_t(w_b[RANK:, :], w_b[...])
    up_half = jnp.where(c == 0, up_part[0:32], up_part[32:64])
    e_buf[t, 32:48, :] = jnp.where(low16, pltpu.roll(up_half[0:16], RANK, 1), up_half[16:32])

    pl.semaphore_wait(barrier, len(everyone))
    drains = []

    def start(phase, src, dst, device):
        remote(src, dst, send_sem.at[phase], recv_sem.at[phase], device).start()

    def spread_to(phase, devices, src, size):
        for device in devices:
            start(phase, src, src, device)
        drains.append((phase, size))

    def sent():
        for phase, size in drains:
            remote(size, size, send_sem.at[phase], recv_sem.at[phase], sibling).wait_send()
        drains.clear()

    def arrived(phase, size):
        remote(size, size, send_sem.at[phase], recv_sem.at[phase], sibling).wait_recv()

    e_size = e_buf.at[pl.ds(0, NT - 1)]
    f_size = f_buf.at[pl.ds(0, NT - 1), pl.ds(0, 17)]
    c_size = c_buf.at[pl.ds(0, NZ - 1)]
    r_size = r_buf.at[pl.ds(0, NYC - 1)]
    spread_to(0, [at_t(p) for p in t_peers], e_buf.at[t], e_size)

    for load in loads[3:7]:
        load.wait()
    for g in range(GROUP):
        q3[pl.ds(g, ROWS, stride=GROUP), :] = q_v[:, g * SIZE : (g + 1) * SIZE].astype(F32)
    pick = (iota((ROWS * GROUP, ROWS), 0) // GROUP == iota((ROWS * GROUP, ROWS), 1)).astype(F32)
    own_key = jnp.dot(pick.astype(BF), nk_v[...], preferred_element_type=F32)
    lengths = jnp.dot(
        (pick * len_v[...].astype(F32)).astype(BF), jnp.ones((ROWS, SIZE), BF), preferred_element_type=F32
    )
    queries = q3[...]
    scale = 1.0 / math.sqrt(SIZE)
    own_score = jnp.sum(queries * own_key, axis=1, keepdims=True) * scale
    onehot = (iota((1, SIZE), 1) == tr_v[...] + 64).astype(F32)
    c_buf[z] = onehot
    loads[7].wait()
    scores = lax.dot_general(
        queries.reshape(ROWS, GROUP, SIZE).astype(BF),
        ck_v[...],
        (((2,), (2,)), ((0,), (0,))),
        preferred_element_type=F32,
    ).reshape(ROWS * GROUP, SIZE)

    live = iota((ROWS * GROUP, SIZE), 1).astype(F32) < lengths
    scores = jnp.where(live, scores * scale, -jnp.inf)
    top = jnp.maximum(jnp.max(scores, axis=1, keepdims=True), own_score)
    weights = jnp.exp(scores - top)
    own_weight = jnp.exp(own_score - top)
    total = jnp.sum(weights, axis=1, keepdims=True) + own_weight
    probs = (weights / total).astype(BF)
    own_prob = (own_weight / total).astype(BF).astype(F32)

    for load in loads[8:]:
        load.wait()
    own_value = jnp.dot(pick.astype(BF), nv_v[...], preferred_element_type=F32)
    context = lax.dot_general(
        probs.reshape(ROWS, GROUP, SIZE),
        cv_v[...],
        (((2,), (1,)), ((0,), (0,))),
        preferred_element_type=F32,
    ).reshape(ROWS * GROUP, SIZE)
    ctx3[...] = context + own_prob * own_value

    squares = jnp.zeros((ROWS, SIZE), F32)
    for g in range(GROUP):
        cols = slice(g * SIZE, (g + 1) * SIZE)
        feature = res_v[:, cols].astype(F32) + ctx3[pl.ds(g, ROWS, stride=GROUP), :]
        squares = squares + feature * feature
        gained = feature * gain_v[:, cols]
        slices[1, g] = gained
        fg_b[:, cols] = gained.astype(BF)
    square_col = jnp.sum(squares, axis=1, keepdims=True)
    eye = iota((ROWS, SIZE), 0) == iota((ROWS, SIZE), 1)
    square_row = jnp.sum(jnp.where(eye, square_col, 0.0), axis=0, keepdims=True)
    feature_part = dot_t(fg_b[...], w_b[...])
    f_buf[t, 0:16, :] = jnp.where(low16, pltpu.roll(feature_part[0:16], RANK, 1), feature_part[16:32])
    f_buf[t, 16:17, :] = square_row
    h_buf[t] = jnp.where(low16, feature_part[0:16], pltpu.roll(feature_part[16:32], RANK, 1))
    spread_to(3, [at_t(p) for p in t_peers], f_buf.at[t, pl.ds(0, 17)], f_size)
    spread_to(1, [at_z(p) for p in z_peers], c_buf.at[z], c_size)
    for p in y_peers:
        start(2, slices.at[0, p], r_buf.at[yc], at_yc(p * 2))
    for p in y_peers:
        start(2, slices.at[1, p], r_buf.at[yc], at_yc(p * 2 + 1))
    start(2, slices.at[1 - c, y], r_buf.at[yc], sibling)
    drains.append((2, r_size))
    r_buf[yc] = slices[c, y]

    arrived(0, e_size)
    u_buf[c] = sum((e_buf[p, 32:48, :] for p in range(1, NT)), e_buf[0, 32:48, :])
    spread_to(13, [sibling], u_buf.at[c], u_buf.at[0])
    early = sum((e_buf[p, 0:32, :] for p in range(1, NT)), e_buf[0, 0:32, :])
    adapter = (early * ROOT).astype(BF).astype(F32)
    a_buf[yc] = jnp.where(low16, adapter[0:16], pltpu.roll(adapter[16:32], RANK, 1))
    for p in y_peers:
        start(4, a_buf.at[yc], a_buf.at[yc], at_yc(p * 2 + 1))
    start(4, a_buf.at[yc], a_buf.at[yc], sibling)
    drains.append((4, a_buf.at[pl.ds(0, NY)]))
    arrived(13, u_buf.at[0])
    ups = jnp.concatenate([pltpu.roll(u_buf[0], RANK, 1), u_buf[0], pltpu.roll(u_buf[1], RANK, 1), u_buf[1]], axis=0)
    spread = jnp.dot(adapter[:, 0:RANK], ups, precision=EXACT, preferred_element_type=F32)
    ahead = early + COEF * spread
    ahead = jnp.where(low16, pltpu.roll(ahead[0:16], RANK, 1), ahead[16:32])
    arrived(1, c_size)
    counts = c_buf[0] + c_buf[1] + c_buf[2] + c_buf[3]
    marks = onehot + pltpu.roll(counts, 32, 1)
    arrived(3, f_size)
    summed = sum((f_buf[p, 0:17, :] for p in range(1, NT)), f_buf[0, 0:17, :])
    rs_row = lax.rsqrt(summed[16:17] * (1.0 / D) + 1e-05)
    rs_col = jnp.sum(jnp.where(eye, rs_row, 0.0), axis=1, keepdims=True)
    l_buf[yc, 0:16, :] = COEF * (ahead - jnp.where(low16, rs_col[0:16], rs_col[16:32]) * summed[0:16])
    l_buf[yc, 16:17, :] = jnp.where(iota((1, SIZE), 1) < ROWS, rs_row, 0.0) + marks
    l_mine = l_buf.at[yc, pl.ds(0, 17)]
    l_row = l_buf.at[yc, pl.ds(16, 1)]
    for p in y_peers:
        start(5, l_mine, l_mine, at_yc(p * 2))
        start(6, l_row, l_row, at_yc(p * 2 + 1))
    start(5, l_mine, l_mine, sibling)
    drains.append((5, l_buf.at[pl.ds(0, NY), pl.ds(0, 17)]))
    drains.append((6, l_buf.at[pl.ds(0, NY - 1), pl.ds(16, 1)]))

    arrived(2, r_size)

    @pl.when(c == 0)
    def _():
        start(7, r_buf, x_buf, sibling)

    spread_to(14, [at_t(p) for p in t_peers], h_buf.at[t], h_buf.at[pl.ds(0, NT - 1)])

    @pl.when(c == 0)
    def _():
        arrived(4, a_buf.at[0])
        arrived(5, l_buf.at[pl.ds(0, NYC - 1), pl.ds(0, 17)])

    @pl.when(c == 1)
    def _():
        arrived(4, a_buf.at[pl.ds(0, NYC - 1)])
        left = a_buf[...].reshape(256, SIZE).astype(BF)
        up = w_b[RANK:, pl.ds(pl.multiple_of(y * SIZE, SIZE), SIZE)]
        none = jnp.zeros_like(up)
        lift_top = jnp.dot(left, jnp.concatenate([up, none], axis=0), preferred_element_type=F32)
        lift_bottom = jnp.dot(left, jnp.concatenate([none, up], axis=0), preferred_element_type=F32)
        arrived(7, x_buf)
        base[0] = x_buf[:, 0:16, :].reshape(256, SIZE) + COEF * lift_top
        base[1] = x_buf[:, 16:32, :].reshape(256, SIZE) + COEF * lift_bottom
        arrived(5, l_buf.at[0, pl.ds(0, 17)])
        arrived(6, l_buf.at[pl.ds(0, NYC - 2), pl.ds(16, 1)])

    rows_of = jnp.broadcast_to(l_buf[:, 16:17, :], (NYC, 16, SIZE))
    lane = iota((NYC, 16, SIZE), 2)
    load_all = pltpu.roll(jnp.sum(l_buf[:, 16:17, :], axis=0), 96, 1)
    load_all = jnp.where(iota((1, SIZE), 1) // 16 == 4, load_all, 0.0)
    weight = 1.0 / (ROWS * jnp.sum(rows_of * load_all[None], axis=2, keepdims=True))

    @pl.when(c == 0)
    def _():
        left = (l_buf[:, 0:16, :] * weight).reshape(256, SIZE).astype(BF)
        top_rows = r_buf[:, 0:16, :].reshape(256, SIZE).astype(BF)
        bottom_rows = r_buf[:, 16:32, :].reshape(256, SIZE).astype(BF)
        z_buf[z] = (dot_rows(left, top_rows)[0:RANK] + dot_rows(left, bottom_rows)[RANK:]) * ROOT

    @pl.when(c == 1)
    def _():
        left = a_buf[...].reshape(256, SIZE).astype(BF)
        place = iota((NYC, 16, SIZE), 1)

        def half(h):
            rs = jnp.sum(jnp.where(lane == place + 16 * h, rows_of, 0.0), axis=2, keepdims=True)
            resid = weight * (base[h].reshape(NYC, 16, SIZE) - rs * r_buf[:, 16 * h : 16 * h + 16, :])
            return dot_rows(left, resid.reshape(256, SIZE).astype(BF))

        z_buf[z] = (half(0)[0:RANK] + half(1)[RANK:]) * COEF

    z_size = z_buf.at[pl.ds(0, NZ - 1)]
    spread_to(8, [at_z(p) for p in z_peers], z_buf.at[z], z_size)
    arrived(14, h_buf.at[pl.ds(0, NT - 1)])
    served = sum((h_buf[p] for p in range(1, NT)), h_buf[0])
    served = jnp.concatenate([served, pltpu.roll(served, RANK, 1)], axis=0)
    serve = (served * rs_col * ROOT).astype(BF)
    drafted = jnp.dot(serve[:, 0:RANK], w_b[RANK:, :], preferred_element_type=F32)
    for g in range(GROUP):
        cols = slice(g * SIZE, (g + 1) * SIZE)
        hidden = (slices[1, g] * rs_col).astype(BF)
        hid_v[:, cols] = hidden
        dn_v[:, cols] = (hidden.astype(F32) + COEF * drafted[:, cols]).astype(BF)


    @pl.when(c == 0)
    def _():
        remote(r_buf, x_buf, send_sem.at[7], recv_sem.at[7], sibling).wait_send()

    sent()
    arrived(8, z_size)
    grad = z_buf[0] + z_buf[1] + z_buf[2] + z_buf[3]
    grads[c, y] = grad

    s_y[y] = jnp.sum(grad * grad, axis=0, keepdims=True)
    own_core = [at_yc(p * 2 + c) for p in y_peers]
    s_size = s_y.at[pl.ds(0, NY - 1)]
    spread_to(9, own_core, s_y.at[y], s_size)
    mine = grads.at[c, y]
    for device in own_core:
        remote(mine, mine, send_sem.at[10], slice_sem.at[y], device).start()
    g_size = grads.at[0, pl.ds(0, NY - 1)]
    drains.append((10, g_size))
    start(11, mine, mine, sibling)
    arrived(9, s_size)
    part = s_y[0]
    for p in range(1, NY):
        part = part + s_y[p]
    place_t = t * 2 + c
    s_t[place_t] = part
    st_size = s_t.at[pl.ds(0, 2 * NT - 1)]
    spread_to(
        12,
        [at_t(p) for p in t_peers] + [(z * NYC + y * 2 + 1 - c, p) for p in t_peers] + [sibling],
        s_t.at[place_t],
        st_size,
    )
    for p in reversed(y_peers):
        piece = grads.at[c, p]
        remote(piece, piece, send_sem.at[10], slice_sem.at[p], sibling).wait_recv()
        start(11, piece, piece, sibling)
    drains.append((11, grads.at[0]))
    arrived(12, st_size)
    whole = s_t[0]
    for p in range(1, 2 * NT):
        whole = whole + s_t[p]
    total_sq = jnp.sum(whole, axis=1, keepdims=True)
    step = 0.5 / jnp.sqrt(total_sq * (1.0 / (2.0 * RANK * D)) + 1e-06)
    @pl.when(c == 0)
    def _():
        for p in range(NY):
            cols = slice(p * SIZE, (p + 1) * SIZE)
            nd_v[:, cols] = fd_v[:, cols] - grads[0, p] * step

    @pl.when(c == 1)
    def _():
        for p in range(NY):
            cols = slice(p * SIZE, (p + 1) * SIZE)
            nu_v[:, cols] = fu_v[:, cols] - grads[1, p] * step

    arrived(11, grads.at[0])

    @pl.when(c == 0)
    def _():
        for p in range(NY):
            cols = slice(p * SIZE, (p + 1) * SIZE)
            nu_v[:, cols] = fu_v[:, cols] - grads[1, p] * step

    @pl.when(c == 1)
    def _():
        for p in range(NY):
            cols = slice(p * SIZE, (p + 1) * SIZE)
            nd_v[:, cols] = fd_v[:, cols] - grads[0, p] * step

    sent()


def hand_over(*refs):
    *refs, sem = refs
    copies = [pltpu.make_async_copy(refs[i], refs[4 + i], sem.at[i]) for i in (2, 3, 0, 1)]
    for copy in copies:
        copy.start()
    for copy in copies:
        copy.wait()


def local(
    queries,
    cache_keys,
    cache_values,
    new_keys,
    new_values,
    cache_lengths,
    residual,
    norm_gain,
    draft_input,
    trainer_of,
    factor_down,
    factor_up,
):
    inputs = (
        queries,
        cache_keys.reshape(ROWS, SIZE, SIZE),
        cache_values.reshape(ROWS, SIZE, SIZE),
        new_keys,
        new_values,
        cache_lengths.reshape(1, ROWS),
        residual,
        norm_gain.reshape(1, WIDTH),
        draft_input,
        trainer_of.reshape(1, 1),
        factor_down,
        factor_up,
    )
    outs = (
        jax.ShapeDtypeStruct((ROWS, WIDTH), BF),
        jax.ShapeDtypeStruct((ROWS, WIDTH), BF),
        jax.ShapeDtypeStruct((RANK, WIDTH), F32),
        jax.ShapeDtypeStruct((RANK, WIDTH), F32),
    )
    vmem = pltpu.VMEM
    dma = pltpu.SemaphoreType.DMA
    scratch = (
        [vmem(a.shape, a.dtype) for a in inputs]
        + [
            vmem((2 * RANK, WIDTH), BF),
            vmem((ROWS * GROUP, SIZE), F32),
            vmem((ROWS * GROUP, SIZE), F32),
            vmem((ROWS, WIDTH), BF),
            vmem((2, NY, ROWS, SIZE), F32),
            vmem((NT, 48, SIZE), F32),
            vmem((2, 16, SIZE), F32),
            vmem((NT, 24, SIZE), F32),
            vmem((NT, 16, SIZE), F32),
            vmem((NYC, ROWS, SIZE), F32),
            vmem((NYC, ROWS, SIZE), F32),
            vmem((NYC, 16, SIZE), F32),
            vmem((NYC, 24, SIZE), F32),
            vmem((2, 256, SIZE), F32),
            vmem((NZ, 1, SIZE), F32),
            vmem((NZ, RANK, SIZE), F32),
            vmem((2, NY, RANK, SIZE), F32),
            vmem((2 * NT, 1, SIZE), F32),
            vmem((NY, 1, SIZE), F32),
            dma((len(inputs),)),
            dma((15,)),
            dma((15,)),
            dma((NY,)),
        ]
    )
    anywhere = pl.BlockSpec(memory_space=pl.ANY)
    results = pl.pallas_call(
        kernel,
        out_shape=tuple(vmem(a.shape, a.dtype) for a in outs),
        in_specs=[anywhere] * len(inputs),
        out_specs=tuple([pl.BlockSpec(memory_space=vmem)] * len(outs)),
        scratch_shapes=scratch,
        compiler_params=pltpu.CompilerParams(
            collective_id=0, has_side_effects=True, vmem_limit_bytes=60 * 1024 * 1024
        ),
        name="decode_and_draft",
    )(*inputs)
    return tuple(
        pl.pallas_call(
            hand_over,
            out_shape=outs,
            in_specs=[pl.BlockSpec(memory_space=vmem)] * len(outs),
            out_specs=tuple([anywhere] * len(outs)),
            scratch_shapes=[dma((len(outs),))],
            compiler_params=pltpu.CompilerParams(vmem_limit_bytes=4 * 1024 * 1024),
            name="hand_over",
        )(*results)
    )


def solution(mesh):
    return jax.shard_map(
        local,
        mesh=mesh,
        in_specs=(
            P("replica", "tensor"),
            P("replica", "tensor", None, None),
            P("replica", "tensor", None, None),
            P("replica", "tensor"),
            P("replica", "tensor"),
            P("replica"),
            P("replica", "tensor"),
            P("tensor"),
            P("replica", "tensor"),
            P("replica"),
            P(None, "tensor"),
            P(None, "tensor"),
        ),
        out_specs=(
            P("replica", "tensor"),
            P("replica", "tensor"),
            P(None, "tensor"),
            P(None, "tensor"),
        ),
        check_vma=False,
    )
```

```python
import functools
import math

import jax
import jax.numpy as jnp
from jax import lax
from jax.experimental import pallas as pl
from jax.experimental.pallas import tpu as pltpu
from jax.sharding import PartitionSpec as P

D = 8192
RANK = 64
ROWS = 32
GROUP = 8
SIZE = 128
WIDTH = 1024
NT = 8
NY = 8
NZ = 4
NYC = 16
ROOT = 1.0 / math.sqrt(D)
COEF = 0.5 / math.sqrt(RANK)
MESH = pl.DeviceIdType.MESH
BF = jnp.bfloat16
F32 = jnp.float32
EXACT = lax.Precision.HIGHEST


def iota(shape, dim):
    return lax.broadcasted_iota(jnp.int32, shape, dim)


def dot_t(a, b):
    return lax.dot_general(a, b, (((1,), (1,)), ((), ())), preferred_element_type=F32)


def dot_rows(a, b):
    return lax.dot_general(a, b, (((0,), (0,)), ((), ())), preferred_element_type=F32)


def remote(src, dst, send_sem, recv_sem, device):
    return pltpu.make_async_remote_copy(
        src_ref=src,
        dst_ref=dst,
        send_sem=send_sem,
        recv_sem=recv_sem,
        device_id=device,
        device_id_type=MESH,
    )


def kernel(
    q_hbm, ck_hbm, cv_hbm, nk_hbm, nv_hbm, len_hbm, res_hbm, gain_hbm, dr_hbm, tr_hbm, fd_hbm, fu_hbm,
    hid_v, dn_v, nd_v, nu_v,
    q_v, ck_v, cv_v, nk_v, nv_v, len_v, res_v, gain_v, dr_v, tr_v, fd_v, fu_v,
    w_b, q3, ctx3, fg_b,
    slices, e_buf, u_buf, f_buf, h_buf, r_buf, x_buf, a_buf, l_buf, base, c_buf, z_buf, grads, s_t, s_y,
    in_sem, send_sem, recv_sem, slice_sem,
):
    r = lax.axis_index("replica")
    t = lax.axis_index("tensor")
    yc = lax.rem(r, NYC)
    z = r // NYC
    y = yc // 2
    c = lax.rem(yc, 2)
    x = t // 2
    low_z = lax.rem(t, 2)
    y_order = (4, 3, 5, 2, 6, 1, 7)
    t_peers = [
        lax.rem(x + dx, 4) * 2 + lax.rem(low_z + dz, 2)
        for dx, dz in ((2, 1), (1, 1), (3, 1), (2, 0), (1, 0), (3, 0), (0, 1))
    ]
    yc_peers = [lax.rem(y + dy, NY) * 2 + lax.rem(c + dc, 2) for dy in y_order for dc in (0, 1)]
    yc_peers = yc_peers + [y * 2 + 1 - c]
    z_peers = [lax.rem(z + dz, NZ) for dz in (2, 1, 3)]
    y_peers = [lax.rem(y + dy, NY) for dy in y_order]

    def at_t(p):
        return (r, p)

    def at_yc(p):
        return (z * NYC + p, t)

    def at_z(p):
        return (p * NYC + yc, t)

    sibling = at_yc(y * 2 + 1 - c)

    barrier = pltpu.get_barrier_semaphore()
    everyone = (
        [at_t(p) for p in t_peers]
        + [at_yc(p) for p in yc_peers]
        + [at_z(p) for p in z_peers]
        + [(z * NYC + y * 2 + 1 - c, p) for p in t_peers]
    )
    for device in everyone:
        pl.semaphore_signal(barrier, inc=1, device_id=device, device_id_type=MESH)

    loads = [
        pltpu.make_async_copy(src, dst, in_sem.at[i])
        for i, (src, dst) in enumerate(
            (
                (fd_hbm, fd_v), (fu_hbm, fu_v), (dr_hbm, dr_v), (q_hbm, q_v), (nk_hbm, nk_v), (len_hbm, len_v),
                (tr_hbm, tr_v), (ck_hbm, ck_v), (cv_hbm, cv_v), (nv_hbm, nv_v), (res_hbm, res_v), (gain_hbm, gain_v),
            )
        )
    ]
    for load in loads:
        load.start()
    for load in loads[:3]:
        load.wait()
    low = iota((ROWS, SIZE), 1) < RANK
    low16 = low[0:16]
    w_b[0:RANK, :] = fd_v[...].astype(BF)
    w_b[RANK:, :] = fu_v[...].astype(BF)
    for g in range(GROUP):
        slices[0, g] = dr_v[:, g * SIZE : (g + 1) * SIZE].astype(F32)
    e_buf[t, 0:32, :] = dot_t(dr_v[...], w_b[...])
    up_part = dot_t(w_b[RANK:, :], w_b[...])
    up_half = jnp.where(c == 0, up_part[0:32], up_part[32:64])
    e_buf[t, 32:48, :] = jnp.where(low16, pltpu.roll(up_half[0:16], RANK, 1), up_half[16:32])

    for load in loads[3:7]:
        load.wait()
    for g in range(GROUP):
        q3[pl.ds(g, ROWS, stride=GROUP), :] = q_v[:, g * SIZE : (g + 1) * SIZE].astype(F32)
    pick = (iota((ROWS * GROUP, ROWS), 0) // GROUP == iota((ROWS * GROUP, ROWS), 1)).astype(F32)
    own_key = jnp.dot(pick.astype(BF), nk_v[...], preferred_element_type=F32)
    lengths = jnp.dot(
        (pick * len_v[...].astype(F32)).astype(BF), jnp.ones((ROWS, SIZE), BF), preferred_element_type=F32
    )
    queries = q3[...]
    scale = 1.0 / math.sqrt(SIZE)
    own_score = jnp.sum(queries * own_key, axis=1, keepdims=True) * scale
    onehot = (iota((1, SIZE), 1) == tr_v[...] + 64).astype(F32)
    c_buf[z] = onehot
    loads[7].wait()
    scores = lax.dot_general(
        queries.reshape(ROWS, GROUP, SIZE).astype(BF),
        ck_v[...],
        (((2,), (2,)), ((0,), (0,))),
        preferred_element_type=F32,
    ).reshape(ROWS * GROUP, SIZE)

    pl.semaphore_wait(barrier, len(everyone))
    drains = []

    def start(phase, src, dst, device):
        remote(src, dst, send_sem.at[phase], recv_sem.at[phase], device).start()

    def spread_to(phase, devices, src, size):
        for device in devices:
            start(phase, src, src, device)
        drains.append((phase, size))

    def sent():
        for phase, size in drains:
            remote(size, size, send_sem.at[phase], recv_sem.at[phase], sibling).wait_send()
        drains.clear()

    def arrived(phase, size):
        remote(size, size, send_sem.at[phase], recv_sem.at[phase], sibling).wait_recv()

    e_size = e_buf.at[pl.ds(0, NT - 1)]
    f_size = f_buf.at[pl.ds(0, NT - 1), pl.ds(0, 17)]
    c_size = c_buf.at[pl.ds(0, NZ - 1)]
    r_size = r_buf.at[pl.ds(0, NYC - 1)]
    spread_to(1, [at_z(p) for p in z_peers], c_buf.at[z], c_size)
    spread_to(0, [at_t(p) for p in t_peers], e_buf.at[t], e_size)
    for p in y_peers:
        start(2, slices.at[0, p], r_buf.at[yc], at_yc(p * 2))

    live = iota((ROWS * GROUP, SIZE), 1).astype(F32) < lengths
    scores = jnp.where(live, scores * scale, -jnp.inf)
    top = jnp.maximum(jnp.max(scores, axis=1, keepdims=True), own_score)
    weights = jnp.exp(scores - top)
    own_weight = jnp.exp(own_score - top)
    total = jnp.sum(weights, axis=1, keepdims=True) + own_weight
    probs = (weights / total).astype(BF)
    own_prob = (own_weight / total).astype(BF).astype(F32)

    for load in loads[8:]:
        load.wait()
    own_value = jnp.dot(pick.astype(BF), nv_v[...], preferred_element_type=F32)
    context = lax.dot_general(
        probs.reshape(ROWS, GROUP, SIZE),
        cv_v[...],
        (((2,), (1,)), ((0,), (0,))),
        preferred_element_type=F32,
    ).reshape(ROWS * GROUP, SIZE)
    ctx3[...] = context + own_prob * own_value

    squares = jnp.zeros((ROWS, SIZE), F32)
    for g in range(GROUP):
        cols = slice(g * SIZE, (g + 1) * SIZE)
        feature = res_v[:, cols].astype(F32) + ctx3[pl.ds(g, ROWS, stride=GROUP), :]
        squares = squares + feature * feature
        gained = feature * gain_v[:, cols]
        slices[1, g] = gained
        fg_b[:, cols] = gained.astype(BF)
    square_col = jnp.sum(squares, axis=1, keepdims=True)
    eye = iota((ROWS, SIZE), 0) == iota((ROWS, SIZE), 1)
    square_row = jnp.sum(jnp.where(eye, square_col, 0.0), axis=0, keepdims=True)
    feature_part = dot_t(fg_b[...], w_b[...])
    f_buf[t, 0:16, :] = jnp.where(low16, pltpu.roll(feature_part[0:16], RANK, 1), feature_part[16:32])
    f_buf[t, 16:17, :] = square_row
    h_buf[t] = jnp.where(low16, feature_part[0:16], pltpu.roll(feature_part[16:32], RANK, 1))
    spread_to(3, [at_t(p) for p in t_peers], f_buf.at[t, pl.ds(0, 17)], f_size)
    for p in y_peers:
        start(2, slices.at[1, p], r_buf.at[yc], at_yc(p * 2 + 1))
    start(2, slices.at[1 - c, y], r_buf.at[yc], sibling)
    drains.append((2, r_size))
    r_buf[yc] = slices[c, y]

    arrived(0, e_size)
    u_buf[c] = sum((e_buf[p, 32:48, :] for p in range(1, NT)), e_buf[0, 32:48, :])
    spread_to(13, [sibling], u_buf.at[c], u_buf.at[0])
    early = sum((e_buf[p, 0:32, :] for p in range(1, NT)), e_buf[0, 0:32, :])
    adapter = (early * ROOT).astype(BF).astype(F32)
    a_buf[yc] = jnp.where(low16, adapter[0:16], pltpu.roll(adapter[16:32], RANK, 1))
    for p in y_peers:
        start(4, a_buf.at[yc], a_buf.at[yc], at_yc(p * 2 + 1))
    start(4, a_buf.at[yc], a_buf.at[yc], sibling)
    drains.append((4, a_buf.at[pl.ds(0, NY)]))
    arrived(13, u_buf.at[0])
    ups = jnp.concatenate([pltpu.roll(u_buf[0], RANK, 1), u_buf[0], pltpu.roll(u_buf[1], RANK, 1), u_buf[1]], axis=0)
    spread = jnp.dot(adapter[:, 0:RANK], ups, precision=EXACT, preferred_element_type=F32)
    ahead = early + COEF * spread
    ahead = jnp.where(low16, pltpu.roll(ahead[0:16], RANK, 1), ahead[16:32])
    arrived(1, c_size)
    counts = c_buf[0] + c_buf[1] + c_buf[2] + c_buf[3]
    marks = onehot + pltpu.roll(counts, 32, 1)
    arrived(3, f_size)
    summed = sum((f_buf[p, 0:17, :] for p in range(1, NT)), f_buf[0, 0:17, :])
    rs_row = lax.rsqrt(summed[16:17] * (1.0 / D) + 1e-05)
    rs_col = jnp.sum(jnp.where(eye, rs_row, 0.0), axis=1, keepdims=True)
    l_buf[yc, 0:16, :] = COEF * (ahead - jnp.where(low16, rs_col[0:16], rs_col[16:32]) * summed[0:16])
    l_buf[yc, 16:17, :] = jnp.where(iota((1, SIZE), 1) < ROWS, rs_row, 0.0) + marks
    l_mine = l_buf.at[yc, pl.ds(0, 17)]
    l_row = l_buf.at[yc, pl.ds(16, 1)]
    for p in y_peers:
        start(5, l_mine, l_mine, at_yc(p * 2))
        start(6, l_row, l_row, at_yc(p * 2 + 1))
    start(5, l_mine, l_mine, sibling)
    drains.append((5, l_buf.at[pl.ds(0, NY), pl.ds(0, 17)]))
    drains.append((6, l_buf.at[pl.ds(0, NY - 1), pl.ds(16, 1)]))

    arrived(2, r_size)

    @pl.when(c == 0)
    def _():
        start(7, r_buf, x_buf, sibling)

    spread_to(14, [at_t(p) for p in t_peers], h_buf.at[t], h_buf.at[pl.ds(0, NT - 1)])

    @pl.when(c == 0)
    def _():
        arrived(4, a_buf.at[0])
        arrived(5, l_buf.at[pl.ds(0, NYC - 1), pl.ds(0, 17)])

    @pl.when(c == 1)
    def _():
        arrived(4, a_buf.at[pl.ds(0, NYC - 1)])
        left = a_buf[...].reshape(256, SIZE).astype(BF)
        up = w_b[RANK:, pl.ds(pl.multiple_of(y * SIZE, SIZE), SIZE)]
        none = jnp.zeros_like(up)
        lift_top = jnp.dot(left, jnp.concatenate([up, none], axis=0), preferred_element_type=F32)
        lift_bottom = jnp.dot(left, jnp.concatenate([none, up], axis=0), preferred_element_type=F32)
        arrived(7, x_buf)
        base[0] = x_buf[:, 0:16, :].reshape(256, SIZE) + COEF * lift_top
        base[1] = x_buf[:, 16:32, :].reshape(256, SIZE) + COEF * lift_bottom
        arrived(5, l_buf.at[0, pl.ds(0, 17)])
        arrived(6, l_buf.at[pl.ds(0, NYC - 2), pl.ds(16, 1)])

    rows_of = jnp.broadcast_to(l_buf[:, 16:17, :], (NYC, 16, SIZE))
    lane = iota((NYC, 16, SIZE), 2)
    load_all = pltpu.roll(jnp.sum(l_buf[:, 16:17, :], axis=0), 96, 1)
    load_all = jnp.where(iota((1, SIZE), 1) // 16 == 4, load_all, 0.0)
    weight = 1.0 / (ROWS * jnp.sum(rows_of * load_all[None], axis=2, keepdims=True))

    @pl.when(c == 0)
    def _():
        left = (l_buf[:, 0:16, :] * weight).reshape(256, SIZE).astype(BF)
        top_rows = r_buf[:, 0:16, :].reshape(256, SIZE).astype(BF)
        bottom_rows = r_buf[:, 16:32, :].reshape(256, SIZE).astype(BF)
        z_buf[z] = (dot_rows(left, top_rows)[0:RANK] + dot_rows(left, bottom_rows)[RANK:]) * ROOT

    @pl.when(c == 1)
    def _():
        left = a_buf[...].reshape(256, SIZE).astype(BF)
        place = iota((NYC, 16, SIZE), 1)

        def half(h):
            rs = jnp.sum(jnp.where(lane == place + 16 * h, rows_of, 0.0), axis=2, keepdims=True)
            resid = weight * (base[h].reshape(NYC, 16, SIZE) - rs * r_buf[:, 16 * h : 16 * h + 16, :])
            return dot_rows(left, resid.reshape(256, SIZE).astype(BF))

        z_buf[z] = (half(0)[0:RANK] + half(1)[RANK:]) * COEF

    z_size = z_buf.at[pl.ds(0, NZ - 1)]
    spread_to(8, [at_z(p) for p in z_peers], z_buf.at[z], z_size)
    arrived(14, h_buf.at[pl.ds(0, NT - 1)])
    served = sum((h_buf[p] for p in range(1, NT)), h_buf[0])
    served = jnp.concatenate([served, pltpu.roll(served, RANK, 1)], axis=0)
    serve = (served * rs_col * ROOT).astype(BF)
    drafted = jnp.dot(serve[:, 0:RANK], w_b[RANK:, :], preferred_element_type=F32)
    for g in range(GROUP):
        cols = slice(g * SIZE, (g + 1) * SIZE)
        hidden = (slices[1, g] * rs_col).astype(BF)
        hid_v[:, cols] = hidden
        dn_v[:, cols] = (hidden.astype(F32) + COEF * drafted[:, cols]).astype(BF)


    @pl.when(c == 0)
    def _():
        remote(r_buf, x_buf, send_sem.at[7], recv_sem.at[7], sibling).wait_send()

    sent()
    arrived(8, z_size)
    grad = z_buf[0] + z_buf[1] + z_buf[2] + z_buf[3]
    grads[c, y] = grad

    s_y[y] = jnp.sum(grad * grad, axis=0, keepdims=True)
    own_core = [at_yc(p * 2 + c) for p in y_peers]
    s_size = s_y.at[pl.ds(0, NY - 1)]
    spread_to(9, own_core, s_y.at[y], s_size)
    mine = grads.at[c, y]
    for device in own_core:
        remote(mine, mine, send_sem.at[10], slice_sem.at[y], device).start()
    g_size = grads.at[0, pl.ds(0, NY - 1)]
    drains.append((10, g_size))
    start(11, mine, mine, sibling)
    arrived(9, s_size)
    part = s_y[0]
    for p in range(1, NY):
        part = part + s_y[p]
    place_t = t * 2 + c
    s_t[place_t] = part
    st_size = s_t.at[pl.ds(0, 2 * NT - 1)]
    spread_to(
        12,
        [at_t(p) for p in t_peers] + [(z * NYC + y * 2 + 1 - c, p) for p in t_peers] + [sibling],
        s_t.at[place_t],
        st_size,
    )
    for p in reversed(y_peers):
        piece = grads.at[c, p]
        remote(piece, piece, send_sem.at[10], slice_sem.at[p], sibling).wait_recv()
        start(11, piece, piece, sibling)
    drains.append((11, grads.at[0]))
    arrived(12, st_size)
    whole = s_t[0]
    for p in range(1, 2 * NT):
        whole = whole + s_t[p]
    total_sq = jnp.sum(whole, axis=1, keepdims=True)
    step = 0.5 / jnp.sqrt(total_sq * (1.0 / (2.0 * RANK * D)) + 1e-06)
    @pl.when(c == 0)
    def _():
        for p in range(NY):
            cols = slice(p * SIZE, (p + 1) * SIZE)
            nd_v[:, cols] = fd_v[:, cols] - grads[0, p] * step

    @pl.when(c == 1)
    def _():
        for p in range(NY):
            cols = slice(p * SIZE, (p + 1) * SIZE)
            nu_v[:, cols] = fu_v[:, cols] - grads[1, p] * step

    arrived(11, grads.at[0])

    @pl.when(c == 0)
    def _():
        for p in range(NY):
            cols = slice(p * SIZE, (p + 1) * SIZE)
            nu_v[:, cols] = fu_v[:, cols] - grads[1, p] * step

    @pl.when(c == 1)
    def _():
        for p in range(NY):
            cols = slice(p * SIZE, (p + 1) * SIZE)
            nd_v[:, cols] = fd_v[:, cols] - grads[0, p] * step

    sent()


def hand_over(*refs):
    *refs, sem = refs
    copies = [pltpu.make_async_copy(refs[i], refs[4 + i], sem.at[i]) for i in (2, 3, 0, 1)]
    for copy in copies:
        copy.start()
    for copy in copies:
        copy.wait()


def local(
    queries,
    cache_keys,
    cache_values,
    new_keys,
    new_values,
    cache_lengths,
    residual,
    norm_gain,
    draft_input,
    trainer_of,
    factor_down,
    factor_up,
):
    inputs = (
        queries,
        cache_keys.reshape(ROWS, SIZE, SIZE),
        cache_values.reshape(ROWS, SIZE, SIZE),
        new_keys,
        new_values,
        cache_lengths.reshape(1, ROWS),
        residual,
        norm_gain.reshape(1, WIDTH),
        draft_input,
        trainer_of.reshape(1, 1),
        factor_down,
        factor_up,
    )
    outs = (
        jax.ShapeDtypeStruct((ROWS, WIDTH), BF),
        jax.ShapeDtypeStruct((ROWS, WIDTH), BF),
        jax.ShapeDtypeStruct((RANK, WIDTH), F32),
        jax.ShapeDtypeStruct((RANK, WIDTH), F32),
    )
    vmem = pltpu.VMEM
    dma = pltpu.SemaphoreType.DMA
    scratch = (
        [vmem(a.shape, a.dtype) for a in inputs]
        + [
            vmem((2 * RANK, WIDTH), BF),
            vmem((ROWS * GROUP, SIZE), F32),
            vmem((ROWS * GROUP, SIZE), F32),
            vmem((ROWS, WIDTH), BF),
            vmem((2, NY, ROWS, SIZE), F32),
            vmem((NT, 48, SIZE), F32),
            vmem((2, 16, SIZE), F32),
            vmem((NT, 24, SIZE), F32),
            vmem((NT, 16, SIZE), F32),
            vmem((NYC, ROWS, SIZE), F32),
            vmem((NYC, ROWS, SIZE), F32),
            vmem((NYC, 16, SIZE), F32),
            vmem((NYC, 24, SIZE), F32),
            vmem((2, 256, SIZE), F32),
            vmem((NZ, 1, SIZE), F32),
            vmem((NZ, RANK, SIZE), F32),
            vmem((2, NY, RANK, SIZE), F32),
            vmem((2 * NT, 1, SIZE), F32),
            vmem((NY, 1, SIZE), F32),
            dma((len(inputs),)),
            dma((15,)),
            dma((15,)),
            dma((NY,)),
        ]
    )
    anywhere = pl.BlockSpec(memory_space=pl.ANY)
    results = pl.pallas_call(
        kernel,
        out_shape=tuple(vmem(a.shape, a.dtype) for a in outs),
        in_specs=[anywhere] * len(inputs),
        out_specs=tuple([pl.BlockSpec(memory_space=vmem)] * len(outs)),
        scratch_shapes=scratch,
        compiler_params=pltpu.CompilerParams(
            collective_id=0, has_side_effects=True, vmem_limit_bytes=60 * 1024 * 1024
        ),
        name="decode_and_draft",
    )(*inputs)
    return tuple(
        pl.pallas_call(
            hand_over,
            out_shape=outs,
            in_specs=[pl.BlockSpec(memory_space=vmem)] * len(outs),
            out_specs=tuple([anywhere] * len(outs)),
            scratch_shapes=[dma((len(outs),))],
            compiler_params=pltpu.CompilerParams(vmem_limit_bytes=4 * 1024 * 1024),
            name="hand_over",
        )(*results)
    )


def solution(mesh):
    return jax.shard_map(
        local,
        mesh=mesh,
        in_specs=(
            P("replica", "tensor"),
            P("replica", "tensor", None, None),
            P("replica", "tensor", None, None),
            P("replica", "tensor"),
            P("replica", "tensor"),
            P("replica"),
            P("replica", "tensor"),
            P("tensor"),
            P("replica", "tensor"),
            P("replica"),
            P(None, "tensor"),
            P(None, "tensor"),
        ),
        out_specs=(
            P("replica", "tensor"),
            P("replica", "tensor"),
            P(None, "tensor"),
            P(None, "tensor"),
        ),
        check_vma=False,
    )
```

```python
import functools
import math

import jax
import jax.numpy as jnp
from jax import lax
from jax.experimental import pallas as pl
from jax.experimental.pallas import tpu as pltpu
from jax.sharding import PartitionSpec as P

D = 8192
RANK = 64
ROWS = 32
GROUP = 8
SIZE = 128
WIDTH = 1024
NT = 8
NY = 8
NZ = 4
NYC = 16
ROOT = 1.0 / math.sqrt(D)
COEF = 0.5 / math.sqrt(RANK)
MESH = pl.DeviceIdType.MESH
BF = jnp.bfloat16
F32 = jnp.float32
EXACT = lax.Precision.HIGHEST


def iota(shape, dim):
    return lax.broadcasted_iota(jnp.int32, shape, dim)


def dot_t(a, b):
    return lax.dot_general(a, b, (((1,), (1,)), ((), ())), preferred_element_type=F32)


def dot_rows(a, b):
    return lax.dot_general(a, b, (((0,), (0,)), ((), ())), preferred_element_type=F32)


def remote(src, dst, send_sem, recv_sem, device):
    return pltpu.make_async_remote_copy(
        src_ref=src,
        dst_ref=dst,
        send_sem=send_sem,
        recv_sem=recv_sem,
        device_id=device,
        device_id_type=MESH,
    )


def kernel(
    q_hbm, ck_hbm, cv_hbm, nk_hbm, nv_hbm, len_hbm, res_hbm, gain_hbm, dr_hbm, tr_hbm, fd_hbm, fu_hbm,
    hid_v, dn_v, nd_v, nu_v,
    q_v, ck_v, cv_v, nk_v, nv_v, len_v, res_v, gain_v, dr_v, tr_v, fd_v, fu_v,
    w_b, q3, ctx3, fg_b,
    slices, e_buf, u_buf, f_buf, h_buf, r_buf, x_buf, a_buf, l_buf, base, c_buf, z_buf, grads, s_t, s_y,
    in_sem, send_sem, recv_sem, slice_sem,
):
    r = lax.axis_index("replica")
    t = lax.axis_index("tensor")
    yc = lax.rem(r, NYC)
    z = r // NYC
    y = yc // 2
    c = lax.rem(yc, 2)
    x = t // 2
    low_z = lax.rem(t, 2)
    y_order = (4, 3, 5, 2, 6, 1, 7)
    t_peers = [
        lax.rem(x + dx, 4) * 2 + lax.rem(low_z + dz, 2)
        for dx, dz in ((2, 1), (1, 1), (3, 1), (2, 0), (1, 0), (3, 0), (0, 1))
    ]
    yc_peers = [lax.rem(y + dy, NY) * 2 + lax.rem(c + dc, 2) for dy in y_order for dc in (0, 1)]
    yc_peers = yc_peers + [y * 2 + 1 - c]
    z_peers = [lax.rem(z + dz, NZ) for dz in (2, 1, 3)]
    y_peers = [lax.rem(y + dy, NY) for dy in y_order]

    def at_t(p):
        return (r, p)

    def at_yc(p):
        return (z * NYC + p, t)

    def at_z(p):
        return (p * NYC + yc, t)

    sibling = at_yc(y * 2 + 1 - c)

    barrier = pltpu.get_barrier_semaphore()
    everyone = (
        [at_t(p) for p in t_peers]
        + [at_yc(p) for p in yc_peers]
        + [at_z(p) for p in z_peers]
        + [(z * NYC + y * 2 + 1 - c, p) for p in t_peers]
    )
    for device in everyone:
        pl.semaphore_signal(barrier, inc=1, device_id=device, device_id_type=MESH)

    loads = [
        pltpu.make_async_copy(src, dst, in_sem.at[i])
        for i, (src, dst) in enumerate(
            (
                (fd_hbm, fd_v), (fu_hbm, fu_v), (dr_hbm, dr_v), (q_hbm, q_v), (nk_hbm, nk_v), (len_hbm, len_v),
                (tr_hbm, tr_v), (ck_hbm, ck_v), (cv_hbm, cv_v), (nv_hbm, nv_v), (res_hbm, res_v), (gain_hbm, gain_v),
            )
        )
    ]
    for load in loads:
        load.start()
    for load in loads[:3]:
        load.wait()
    low = iota((ROWS, SIZE), 1) < RANK
    low16 = low[0:16]
    w_b[0:RANK, :] = fd_v[...].astype(BF)
    w_b[RANK:, :] = fu_v[...].astype(BF)
    for g in range(GROUP):
        slices[0, g] = dr_v[:, g * SIZE : (g + 1) * SIZE].astype(F32)
    e_buf[t, 0:32, :] = dot_t(dr_v[...], w_b[...])
    up_part = dot_t(w_b[RANK:, :], w_b[...])
    up_half = jnp.where(c == 0, up_part[0:32], up_part[32:64])
    e_buf[t, 32:48, :] = jnp.where(low16, pltpu.roll(up_half[0:16], RANK, 1), up_half[16:32])

    for load in loads[3:7]:
        load.wait()
    for g in range(GROUP):
        q3[pl.ds(g, ROWS, stride=GROUP), :] = q_v[:, g * SIZE : (g + 1) * SIZE].astype(F32)
    pick = (iota((ROWS * GROUP, ROWS), 0) // GROUP == iota((ROWS * GROUP, ROWS), 1)).astype(F32)
    own_key = jnp.dot(pick.astype(BF), nk_v[...], preferred_element_type=F32)
    lengths = jnp.dot(
        (pick * len_v[...].astype(F32)).astype(BF), jnp.ones((ROWS, SIZE), BF), preferred_element_type=F32
    )
    queries = q3[...]
    scale = 1.0 / math.sqrt(SIZE)
    own_score = jnp.sum(queries * own_key, axis=1, keepdims=True) * scale
    onehot = (iota((1, SIZE), 1) == tr_v[...] + 64).astype(F32)
    c_buf[z] = onehot
    loads[7].wait()
    scores = lax.dot_general(
        queries.reshape(ROWS, GROUP, SIZE).astype(BF),
        ck_v[...],
        (((2,), (2,)), ((0,), (0,))),
        preferred_element_type=F32,
    ).reshape(ROWS * GROUP, SIZE)

    pl.semaphore_wait(barrier, len(everyone))
    drains = []

    def start(phase, src, dst, device):
        remote(src, dst, send_sem.at[phase], recv_sem.at[phase], device).start()

    def spread_to(phase, devices, src, size):
        for device in devices:
            start(phase, src, src, device)
        drains.append((phase, size))

    def sent():
        for phase, size in drains:
            remote(size, size, send_sem.at[phase], recv_sem.at[phase], sibling).wait_send()
        drains.clear()

    def arrived(phase, size):
        remote(size, size, send_sem.at[phase], recv_sem.at[phase], sibling).wait_recv()

    e_size = e_buf.at[pl.ds(0, NT - 1)]
    f_size = f_buf.at[pl.ds(0, NT - 1), pl.ds(0, 17)]
    c_size = c_buf.at[pl.ds(0, NZ - 1)]
    r_size = r_buf.at[pl.ds(0, NYC - 1)]
    spread_to(1, [at_z(p) for p in z_peers], c_buf.at[z], c_size)
    spread_to(0, [at_t(p) for p in t_peers], e_buf.at[t], e_size)
    for p in y_peers:
        start(2, slices.at[0, p], r_buf.at[yc], at_yc(p * 2))

    live = iota((ROWS * GROUP, SIZE), 1).astype(F32) < lengths
    scores = jnp.where(live, scores * scale, -jnp.inf)
    top = jnp.maximum(jnp.max(scores, axis=1, keepdims=True), own_score)
    weights = jnp.exp(scores - top)
    own_weight = jnp.exp(own_score - top)
    total = jnp.sum(weights, axis=1, keepdims=True) + own_weight
    probs = (weights / total).astype(BF)
    own_prob = (own_weight / total).astype(BF).astype(F32)

    for load in loads[8:]:
        load.wait()
    own_value = jnp.dot(pick.astype(BF), nv_v[...], preferred_element_type=F32)
    context = lax.dot_general(
        probs.reshape(ROWS, GROUP, SIZE),
        cv_v[...],
        (((2,), (1,)), ((0,), (0,))),
        preferred_element_type=F32,
    ).reshape(ROWS * GROUP, SIZE)
    ctx3[...] = context + own_prob * own_value

    squares = jnp.zeros((ROWS, SIZE), F32)
    for g in range(GROUP):
        cols = slice(g * SIZE, (g + 1) * SIZE)
        feature = res_v[:, cols].astype(F32) + ctx3[pl.ds(g, ROWS, stride=GROUP), :]
        squares = squares + feature * feature
        gained = feature * gain_v[:, cols]
        slices[1, g] = gained
        fg_b[:, cols] = gained.astype(BF)
    square_col = jnp.sum(squares, axis=1, keepdims=True)
    eye = iota((ROWS, SIZE), 0) == iota((ROWS, SIZE), 1)
    square_row = jnp.sum(jnp.where(eye, square_col, 0.0), axis=0, keepdims=True)
    feature_part = dot_t(fg_b[...], w_b[...])
    f_buf[t, 0:16, :] = jnp.where(low16, pltpu.roll(feature_part[0:16], RANK, 1), feature_part[16:32])
    f_buf[t, 16:17, :] = square_row
    h_buf[t] = jnp.where(low16, feature_part[0:16], pltpu.roll(feature_part[16:32], RANK, 1))
    spread_to(3, [at_t(p) for p in t_peers], f_buf.at[t, pl.ds(0, 17)], f_size)
    for p in y_peers:
        start(2, slices.at[1, p], r_buf.at[yc], at_yc(p * 2 + 1))
    start(2, slices.at[1 - c, y], r_buf.at[yc], sibling)
    drains.append((2, r_size))
    r_buf[yc] = slices[c, y]

    arrived(0, e_size)
    u_buf[c] = sum((e_buf[p, 32:48, :] for p in range(1, NT)), e_buf[0, 32:48, :])
    spread_to(13, [sibling], u_buf.at[c], u_buf.at[0])
    early = sum((e_buf[p, 0:32, :] for p in range(1, NT)), e_buf[0, 0:32, :])
    adapter = (early * ROOT).astype(BF).astype(F32)
    a_buf[yc] = jnp.where(low16, adapter[0:16], pltpu.roll(adapter[16:32], RANK, 1))
    for p in y_peers:
        start(4, a_buf.at[yc], a_buf.at[yc], at_yc(p * 2 + 1))
    start(4, a_buf.at[yc], a_buf.at[yc], sibling)
    drains.append((4, a_buf.at[pl.ds(0, NY)]))
    arrived(13, u_buf.at[0])
    ups = jnp.concatenate([pltpu.roll(u_buf[0], RANK, 1), u_buf[0], pltpu.roll(u_buf[1], RANK, 1), u_buf[1]], axis=0)
    spread = jnp.dot(adapter[:, 0:RANK], ups, precision=EXACT, preferred_element_type=F32)
    ahead = early + COEF * spread
    ahead = jnp.where(low16, pltpu.roll(ahead[0:16], RANK, 1), ahead[16:32])
    arrived(1, c_size)
    counts = c_buf[0] + c_buf[1] + c_buf[2] + c_buf[3]
    marks = onehot + pltpu.roll(counts, 32, 1)
    arrived(3, f_size)
    summed = sum((f_buf[p, 0:17, :] for p in range(1, NT)), f_buf[0, 0:17, :])
    rs_row = lax.rsqrt(summed[16:17] * (1.0 / D) + 1e-05)
    rs_col = jnp.sum(jnp.where(eye, rs_row, 0.0), axis=1, keepdims=True)
    l_buf[yc, 0:16, :] = COEF * (ahead - jnp.where(low16, rs_col[0:16], rs_col[16:32]) * summed[0:16])
    l_buf[yc, 16:17, :] = jnp.where(iota((1, SIZE), 1) < ROWS, rs_row, 0.0) + marks
    l_mine = l_buf.at[yc, pl.ds(0, 17)]
    l_row = l_buf.at[yc, pl.ds(16, 1)]
    for p in y_peers:
        start(5, l_mine, l_mine, at_yc(p * 2))
        start(6, l_row, l_row, at_yc(p * 2 + 1))
    start(5, l_mine, l_mine, sibling)
    drains.append((5, l_buf.at[pl.ds(0, NY), pl.ds(0, 17)]))
    drains.append((6, l_buf.at[pl.ds(0, NY - 1), pl.ds(16, 1)]))

    arrived(2, r_size)

    @pl.when(c == 0)
    def _():
        start(7, r_buf, x_buf, sibling)

    spread_to(14, [at_t(p) for p in t_peers], h_buf.at[t], h_buf.at[pl.ds(0, NT - 1)])

    @pl.when(c == 0)
    def _():
        arrived(4, a_buf.at[0])
        arrived(5, l_buf.at[pl.ds(0, NYC - 1), pl.ds(0, 17)])

    @pl.when(c == 1)
    def _():
        arrived(4, a_buf.at[pl.ds(0, NYC - 1)])
        left = a_buf[...].reshape(256, SIZE).astype(BF)
        up = w_b[RANK:, pl.ds(pl.multiple_of(y * SIZE, SIZE), SIZE)]
        none = jnp.zeros_like(up)
        lift_top = jnp.dot(left, jnp.concatenate([up, none], axis=0), preferred_element_type=F32)
        lift_bottom = jnp.dot(left, jnp.concatenate([none, up], axis=0), preferred_element_type=F32)
        arrived(7, x_buf)
        base[0] = x_buf[:, 0:16, :].reshape(256, SIZE) + COEF * lift_top
        base[1] = x_buf[:, 16:32, :].reshape(256, SIZE) + COEF * lift_bottom
        arrived(5, l_buf.at[0, pl.ds(0, 17)])
        arrived(6, l_buf.at[pl.ds(0, NYC - 2), pl.ds(16, 1)])

    rows_of = jnp.broadcast_to(l_buf[:, 16:17, :], (NYC, 16, SIZE))
    lane = iota((NYC, 16, SIZE), 2)
    load_all = pltpu.roll(jnp.sum(l_buf[:, 16:17, :], axis=0), 96, 1)
    load_all = jnp.where(iota((1, SIZE), 1) // 16 == 4, load_all, 0.0)
    weight = 1.0 / (ROWS * jnp.sum(rows_of * load_all[None], axis=2, keepdims=True))

    @pl.when(c == 0)
    def _():
        left = (l_buf[:, 0:16, :] * weight).reshape(256, SIZE).astype(BF)
        top_rows = r_buf[:, 0:16, :].reshape(256, SIZE).astype(BF)
        bottom_rows = r_buf[:, 16:32, :].reshape(256, SIZE).astype(BF)
        z_buf[z] = (dot_rows(left, top_rows)[0:RANK] + dot_rows(left, bottom_rows)[RANK:]) * ROOT

    @pl.when(c == 1)
    def _():
        left = a_buf[...].reshape(256, SIZE).astype(BF)
        place = iota((NYC, 16, SIZE), 1)

        def half(h):
            rs = jnp.sum(jnp.where(lane == place + 16 * h, rows_of, 0.0), axis=2, keepdims=True)
            resid = weight * (base[h].reshape(NYC, 16, SIZE) - rs * r_buf[:, 16 * h : 16 * h + 16, :])
            return dot_rows(left, resid.reshape(256, SIZE).astype(BF))

        z_buf[z] = (half(0)[0:RANK] + half(1)[RANK:]) * COEF

    z_size = z_buf.at[pl.ds(0, NZ - 1)]
    spread_to(8, [at_z(p) for p in z_peers], z_buf.at[z], z_size)
    arrived(14, h_buf.at[pl.ds(0, NT - 1)])
    served = sum((h_buf[p] for p in range(1, NT)), h_buf[0])
    served = jnp.concatenate([served, pltpu.roll(served, RANK, 1)], axis=0)
    serve = (served * rs_col * ROOT).astype(BF)
    drafted = jnp.dot(serve[:, 0:RANK], w_b[RANK:, :], preferred_element_type=F32)
    for g in range(GROUP):
        cols = slice(g * SIZE, (g + 1) * SIZE)
        hidden = (slices[1, g] * rs_col).astype(BF)
        hid_v[:, cols] = hidden
        dn_v[:, cols] = (hidden.astype(F32) + COEF * drafted[:, cols]).astype(BF)


    @pl.when(c == 0)
    def _():
        remote(r_buf, x_buf, send_sem.at[7], recv_sem.at[7], sibling).wait_send()

    sent()
    arrived(8, z_size)
    grad = z_buf[0] + z_buf[1] + z_buf[2] + z_buf[3]
    grads[c, y] = grad

    place_t = t * 2 + c
    s_t[place_t] = jnp.sum(grad * grad, axis=0, keepdims=True)
    st_size = s_t.at[pl.ds(0, 2 * NT - 1)]
    spread_to(
        12,
        [at_t(p) for p in t_peers] + [(z * NYC + y * 2 + 1 - c, p) for p in t_peers] + [sibling],
        s_t.at[place_t],
        st_size,
    )
    own_core = [at_yc(p * 2 + c) for p in y_peers]
    mine = grads.at[c, y]
    for device in own_core:
        remote(mine, mine, send_sem.at[10], slice_sem.at[y], device).start()
    g_size = grads.at[0, pl.ds(0, NY - 1)]
    drains.append((10, g_size))
    start(11, mine, mine, sibling)
    arrived(12, st_size)
    part = s_t[0]
    for p in range(1, 2 * NT):
        part = part + s_t[p]
    s_y[y] = part
    s_size = s_y.at[pl.ds(0, NY - 1)]
    spread_to(9, own_core, s_y.at[y], s_size)
    for p in reversed(y_peers):
        piece = grads.at[c, p]
        remote(piece, piece, send_sem.at[10], slice_sem.at[p], sibling).wait_recv()
        start(11, piece, piece, sibling)
    drains.append((11, grads.at[0]))
    arrived(9, s_size)
    whole = s_y[0]
    for p in range(1, NY):
        whole = whole + s_y[p]
    total_sq = jnp.sum(whole, axis=1, keepdims=True)
    step = 0.5 / jnp.sqrt(total_sq * (1.0 / (2.0 * RANK * D)) + 1e-06)
    @pl.when(c == 0)
    def _():
        for p in range(NY):
            cols = slice(p * SIZE, (p + 1) * SIZE)
            nd_v[:, cols] = fd_v[:, cols] - grads[0, p] * step

    @pl.when(c == 1)
    def _():
        for p in range(NY):
            cols = slice(p * SIZE, (p + 1) * SIZE)
            nu_v[:, cols] = fu_v[:, cols] - grads[1, p] * step

    arrived(11, grads.at[0])

    @pl.when(c == 0)
    def _():
        for p in range(NY):
            cols = slice(p * SIZE, (p + 1) * SIZE)
            nu_v[:, cols] = fu_v[:, cols] - grads[1, p] * step

    @pl.when(c == 1)
    def _():
        for p in range(NY):
            cols = slice(p * SIZE, (p + 1) * SIZE)
            nd_v[:, cols] = fd_v[:, cols] - grads[0, p] * step

    sent()


def hand_over(*refs):
    *refs, sem = refs
    copies = [pltpu.make_async_copy(refs[i], refs[4 + i], sem.at[i]) for i in (2, 3, 0, 1)]
    for copy in copies:
        copy.start()
    for copy in copies:
        copy.wait()


def local(
    queries,
    cache_keys,
    cache_values,
    new_keys,
    new_values,
    cache_lengths,
    residual,
    norm_gain,
    draft_input,
    trainer_of,
    factor_down,
    factor_up,
):
    inputs = (
        queries,
        cache_keys.reshape(ROWS, SIZE, SIZE),
        cache_values.reshape(ROWS, SIZE, SIZE),
        new_keys,
        new_values,
        cache_lengths.reshape(1, ROWS),
        residual,
        norm_gain.reshape(1, WIDTH),
        draft_input,
        trainer_of.reshape(1, 1),
        factor_down,
        factor_up,
    )
    outs = (
        jax.ShapeDtypeStruct((ROWS, WIDTH), BF),
        jax.ShapeDtypeStruct((ROWS, WIDTH), BF),
        jax.ShapeDtypeStruct((RANK, WIDTH), F32),
        jax.ShapeDtypeStruct((RANK, WIDTH), F32),
    )
    vmem = pltpu.VMEM
    dma = pltpu.SemaphoreType.DMA
    scratch = (
        [vmem(a.shape, a.dtype) for a in inputs]
        + [
            vmem((2 * RANK, WIDTH), BF),
            vmem((ROWS * GROUP, SIZE), F32),
            vmem((ROWS * GROUP, SIZE), F32),
            vmem((ROWS, WIDTH), BF),
            vmem((2, NY, ROWS, SIZE), F32),
            vmem((NT, 48, SIZE), F32),
            vmem((2, 16, SIZE), F32),
            vmem((NT, 24, SIZE), F32),
            vmem((NT, 16, SIZE), F32),
            vmem((NYC, ROWS, SIZE), F32),
            vmem((NYC, ROWS, SIZE), F32),
            vmem((NYC, 16, SIZE), F32),
            vmem((NYC, 24, SIZE), F32),
            vmem((2, 256, SIZE), F32),
            vmem((NZ, 1, SIZE), F32),
            vmem((NZ, RANK, SIZE), F32),
            vmem((2, NY, RANK, SIZE), F32),
            vmem((2 * NT, 1, SIZE), F32),
            vmem((NY, 1, SIZE), F32),
            dma((len(inputs),)),
            dma((15,)),
            dma((15,)),
            dma((NY,)),
        ]
    )
    anywhere = pl.BlockSpec(memory_space=pl.ANY)
    results = pl.pallas_call(
        kernel,
        out_shape=tuple(vmem(a.shape, a.dtype) for a in outs),
        in_specs=[anywhere] * len(inputs),
        out_specs=tuple([pl.BlockSpec(memory_space=vmem)] * len(outs)),
        scratch_shapes=scratch,
        compiler_params=pltpu.CompilerParams(
            collective_id=0, has_side_effects=True, vmem_limit_bytes=60 * 1024 * 1024
        ),
        name="decode_and_draft",
    )(*inputs)
    return tuple(
        pl.pallas_call(
            hand_over,
            out_shape=outs,
            in_specs=[pl.BlockSpec(memory_space=vmem)] * len(outs),
            out_specs=tuple([anywhere] * len(outs)),
            scratch_shapes=[dma((len(outs),))],
            compiler_params=pltpu.CompilerParams(vmem_limit_bytes=4 * 1024 * 1024),
            name="hand_over",
        )(*results)
    )


def solution(mesh):
    return jax.shard_map(
        local,
        mesh=mesh,
        in_specs=(
            P("replica", "tensor"),
            P("replica", "tensor", None, None),
            P("replica", "tensor", None, None),
            P("replica", "tensor"),
            P("replica", "tensor"),
            P("replica"),
            P("replica", "tensor"),
            P("tensor"),
            P("replica", "tensor"),
            P("replica"),
            P(None, "tensor"),
            P(None, "tensor"),
        ),
        out_specs=(
            P("replica", "tensor"),
            P("replica", "tensor"),
            P(None, "tensor"),
            P(None, "tensor"),
        ),
        check_vma=False,
    )
```
